32 devices in a mesh: groups: 2 (over y), ctx: 4 (over z), dp: 2 (over x), sub: 2 (over core).
Axes of the slice: x: 2, y: 2, z: 4, core: 2. Of those that a mesh axis runs over, the one named last changes fastest.
Arguments:
- q_glob: bfloat16 [1024, 2048], P(('groups', 'ctx'), ('dp', 'sub')), parts along dimension 0, may hold values from -6 to 6
- k_glob: bfloat16 [1024, 2048], P(('groups', 'ctx'), ('dp', 'sub')), parts along dimension 0, may hold values from -6 to 6
- v_glob: bfloat16 [1024, 2048], P(('groups', 'ctx'), ('dp', 'sub')), parts along dimension 0, may hold values from -6 to 6
- x_glob: bfloat16 [1024, 4096], P(('groups', 'ctx'), ('dp', 'sub')), parts along dimension 0, may hold values from -0.049804688 to 0.049804688
- out_weight: bfloat16 [2048, 4096], P(('dp', 'sub')), may hold values from -0.125 to 0.125
- bridge_weight: bfloat16 [512, 1024], P(('dp', 'sub')), may hold values from -0.25 to 0.25
- byte_embed: bfloat16 [1024, 8, 1024], P(('groups', 'ctx', 'dp', 'sub')), parts along dimension 0, may hold values from -0.049804688 to 0.049804688
- norm_gain: float32 [1024], replicated, may hold values from 0.1 to 1.9
- qkv_weight: bfloat16 [1024, 3072], P(None, ('dp', 'sub')), may hold values from -0.1875 to 0.1875
Outputs:
- local_qkv: bfloat16 [1024, 8, 3072], P(('groups', 'ctx', 'dp', 'sub')), parts along dimension 0
The draws below stay inside these ranges and needn't reach their ends.
There are 2 independent parts, one for each index of `groups`. The reference program is written for one: setup_inputs(seed, part) draws one part's arguments, and reference() takes and returns one part's arrays. A program takes and returns all parts, laid end to end along the dimension named above; an argument that names none is the same for every part. Nothing has to cross between parts.
All inputs are finite; a program needn't handle non-finite values.
Results may differ from the reference program's by a relative error of at most 0.024.
Values may be sent and summed in bfloat16 or wider, within the bound.
No kernel may reach another device: no remote copies, remote signals or barrier semaphores. Data moves between devices by JAX's collectives and lax.ppermute only.
A program may use at most 64 MiB of HBM per device.

```python
import math
import jax
import jax.numpy as jnp
from jax import lax

DG = 4096
GH = 16
HD = 128
DL = 1024
P_SIZE = 8
PATCHES = 512
DSLICE = 512


def draw_q_glob(key, part):
    key = jax.random.fold_in(key, 7)
    values = jnp.clip(jax.random.normal(key, (PATCHES, GH * HD), jnp.float32), -6.0, 6.0)
    return values.astype(jnp.bfloat16)


def draw_k_glob(key, part):
    key = jax.random.fold_in(key, 13)
    values = jnp.clip(jax.random.normal(key, (PATCHES, GH * HD), jnp.float32), -6.0, 6.0)
    return values.astype(jnp.bfloat16)


def levels(own_key, shape, cuts, smallest, high):
    gain = 1.0
    for dim, parts in cuts:
        heights = jax.random.uniform(jax.random.fold_in(jax.random.fold_in(own_key, 6), dim), (parts,), jnp.float32, smallest / len(cuts), high / len(cuts))
        gain = gain * jnp.repeat(jnp.exp(heights), shape[dim] // parts).reshape((-1,) + (1,) * (len(shape) - 1 - dim))
    return gain


def centred(key, dims, scale, limit, shards=(), held_as=jnp.bfloat16):
    result = jax.random.normal(key, dims, jnp.float32) * scale
    if len(shards) > 0:
        result = levels(key, dims, shards, -0.22, 0.18) * result
    return jnp.clip(result, min=-limit, max=limit).astype(held_as)


def setup_inputs(seed: int = 0, part: int = 0) -> dict:
    streams_of = jax.random.split(jax.random.key(seed), 10)
    own_keys = jax.random.split(jax.random.fold_in(streams_of[9], part), 10)
    q_glob = draw_q_glob(jax.random.fold_in(jax.random.fold_in(streams_of[9], part), 71), part)
    k_glob = draw_k_glob(jax.random.fold_in(jax.random.fold_in(streams_of[9], part), 71), part)
    v_glob = centred(own_keys[2], (PATCHES, GH * HD), 1.0, 6.0, ((0, 4), (1, 4)))
    x_glob = jnp.clip(jax.random.uniform(own_keys[3], (PATCHES, DG), jnp.float32, -0.049804688, 0.049804688) * levels(own_keys[3], (PATCHES, DG), ((0, 4), (1, 4)), -0.4, 0.0), -0.049804688, 0.049804688).astype(jnp.bfloat16)
    out_weight = centred(streams_of[4], (GH * HD, DG), (GH * HD) ** -0.5, 0.125, ((0, 4),))
    bridge_weight = centred(streams_of[5], (DSLICE, DL), DSLICE ** -0.5, 0.25, ((0, 4),))
    byte_embed = jnp.clip(jax.random.uniform(own_keys[6], (PATCHES, P_SIZE, DL), jnp.float32, -0.049804688, 0.049804688) * levels(own_keys[6], (PATCHES, P_SIZE, DL), ((0, 16),), -0.4, 0.0), -0.049804688, 0.049804688).astype(jnp.bfloat16)
    norm_gain = jnp.clip(1.0 + 0.18 * jax.random.normal(streams_of[7], (DL,), jnp.float32), 0.1, 1.9)
    qkv_weight = centred(streams_of[8], (DL, 3 * DL), DL ** -0.5, 0.1875, ((1, 4),))
    return dict(q_glob=q_glob, k_glob=k_glob, v_glob=v_glob, x_glob=x_glob, out_weight=out_weight, bridge_weight=bridge_weight, byte_embed=byte_embed, norm_gain=norm_gain, qkv_weight=qkv_weight)


def reference(q_glob, k_glob, v_glob, x_glob, out_weight, bridge_weight, byte_embed, norm_gain, qkv_weight):
    score_scale = 1.0 / math.sqrt(HD)
    positions = jnp.arange(PATCHES, dtype=jnp.int32)
    causal = positions[:, None] >= positions[None, :]
    queries = q_glob.reshape(PATCHES, GH, HD).transpose(1, 0, 2)
    keys = k_glob.reshape(PATCHES, GH, HD).transpose(1, 0, 2)
    values = v_glob.reshape(PATCHES, GH, HD).transpose(1, 0, 2)

    def one_head(operands):
        query_head, key_head, value_head = operands
        scores = jnp.dot(query_head, key_head.T, preferred_element_type=jnp.float32) * score_scale
        scores = jnp.where(causal, scores, -jnp.inf)
        row_max = lax.optimization_barrier(jnp.max(scores, axis=1, keepdims=True))
        weights = jnp.exp(scores - row_max)
        row_sum = lax.optimization_barrier(jnp.sum(weights, axis=1, keepdims=True))
        mixed = jnp.dot(weights.astype(jnp.bfloat16), value_head, preferred_element_type=jnp.float32)
        return (mixed / row_sum).astype(jnp.bfloat16)
    attn = lax.map(one_head, (queries, keys, values))
    attn = attn.transpose(1, 0, 2).reshape(PATCHES, GH * HD)
    glob_out = (x_glob.astype(jnp.float32) + jnp.dot(attn, out_weight, preferred_element_type=jnp.float32)).astype(jnp.bfloat16)
    glob_bytes = glob_out.reshape(PATCHES * P_SIZE, DSLICE)
    byte_in = byte_embed.reshape(PATCHES * P_SIZE, DL).astype(jnp.float32) + jnp.dot(glob_bytes, bridge_weight, preferred_element_type=jnp.float32)
    mean_square = lax.optimization_barrier(jnp.mean(byte_in * byte_in, axis=1, keepdims=True))
    normalized = (byte_in * lax.rsqrt(mean_square + 1e-05) * norm_gain.astype(jnp.float32)).astype(jnp.bfloat16)
    local_qkv = jnp.dot(normalized, qkv_weight, preferred_element_type=jnp.float32).astype(jnp.bfloat16)
    return local_qkv.reshape(PATCHES, P_SIZE, 3 * DL)
```

```python
import functools
import math

import jax
import jax.numpy as jnp
from jax import lax
from jax.experimental import pallas as pl
from jax.experimental.pallas import tpu as pltpu
from jax.sharding import PartitionSpec as P

HD = 128
DL = 1024
P_SIZE = 8
DSLICE = 512
GROUP = ("dp", "sub")
SCALE = 1.0 / math.sqrt(HD)
VMEM = pl.BlockSpec(memory_space=pltpu.VMEM)
SMEM = pl.BlockSpec(memory_space=pltpu.SMEM)
F32 = jnp.float32
BF16 = jnp.bfloat16


def dot(a, b):
    return jnp.dot(a, b, preferred_element_type=F32)


def any_mesh(
    q_glob, k_glob, v_glob, x_glob, out_weight, bridge_weight, byte_embed, norm_gain, qkv_weight
):
    query_rows, query_width = q_glob.shape
    head_count = query_width // HD
    first_row = lax.axis_index("ctx") * query_rows
    queries = q_glob.reshape(query_rows, head_count, HD)
    query_pos = first_row + lax.iota(jnp.int32, query_rows)
    keys = lax.all_gather(k_glob, "ctx", axis=0, tiled=True)
    values = lax.all_gather(v_glob, "ctx", axis=0, tiled=True)
    count = keys.shape[0]
    keys = keys.reshape(count, head_count, HD)
    values = values.reshape(count, head_count, HD)
    scores = jnp.einsum("qhd,khd->hqk", queries, keys, preferred_element_type=F32) * SCALE
    allowed = query_pos[:, None] >= lax.iota(jnp.int32, count)[None, :]
    scores = jnp.where(allowed[None], scores, -jnp.inf)
    weights = jnp.exp(scores - jnp.max(scores, axis=2)[:, :, None])
    row_sum = jnp.sum(weights, axis=2)
    weighted = jnp.einsum("hqk,khd->hqd", weights.astype(BF16), values, preferred_element_type=F32)
    attn = (weighted / row_sum[:, :, None]).astype(BF16)
    attn = attn.transpose(1, 0, 2).reshape(query_rows, query_width)
    head_terms = dot(attn, out_weight)
    own_bytes = P_SIZE // lax.axis_size(GROUP)
    feature_sum = lax.psum_scatter(
        head_terms.astype(BF16), GROUP, scatter_dimension=1, tiled=True
    ).astype(F32)
    patch_out = (feature_sum + x_glob.astype(F32)).astype(BF16)
    patch_out = patch_out.reshape(query_rows, own_bytes, DSLICE)
    patch_out = lax.all_to_all(patch_out, GROUP, split_axis=0, concat_axis=1, tiled=True)
    glob_bytes = patch_out.reshape(-1, DSLICE)
    byte_rows = glob_bytes.shape[0]
    bridged = dot(glob_bytes, lax.all_gather(bridge_weight, GROUP, axis=0, tiled=True))
    byte_in = byte_embed.reshape(byte_rows, DL).astype(F32) + bridged
    mean_square = jnp.mean(byte_in * byte_in, axis=1, keepdims=True)
    normalized = (byte_in * lax.rsqrt(mean_square + 1e-05) * norm_gain).astype(BF16)
    result = dot(normalized, lax.all_gather(qkv_weight, GROUP, axis=1, tiled=True)).astype(BF16)
    return result.reshape(byte_embed.shape[0], P_SIZE, 3 * DL)


def attend_project_kernel(
    place, q, x, w, *refs, heads, blocks
):
    keys, values = refs[:blocks], refs[blocks : 2 * blocks]
    away, kept, attn, xs = refs[2 * blocks :]
    ctx, dp, sub = place[0], place[1], place[2]
    rows = q.shape[0]
    quarter = rows // 4
    row = lax.broadcasted_iota(jnp.int32, (rows, rows), 0)
    col = lax.broadcasted_iota(jnp.int32, (rows, rows), 1)
    for h in range(heads):
        cols = pl.ds(h * HD, HD)
        qh = q[:, cols]
        scores = []
        for s in range(blocks):
            sc = lax.dot_general(
                qh, keys[s][:, cols], (((1,), (1,)), ((), ())), preferred_element_type=F32
            ) * SCALE
            keep = (row >= col) if s == 0 else (ctx >= s)
            scores.append(jnp.where(keep, sc, -jnp.inf))
        scores = jnp.concatenate(scores, axis=1)
        probs = jnp.exp(scores - jnp.max(scores, axis=1, keepdims=True))
        total = jnp.sum(probs, axis=1, keepdims=True)
        probs = probs.astype(BF16)
        mixed = dot(probs[:, :rows], values[0][:, cols])
        for s in range(1, blocks):
            mixed += dot(probs[:, s * rows : (s + 1) * rows], values[s][:, cols])
        attn[:, cols] = (mixed / total).astype(BF16)
    order = []
    for core in (1 - sub, sub):
        for chip in (1 - dp, dp):
            order.append(pl.ds(pl.multiple_of((chip * 2 + core) * quarter, quarter), quarter))
    a = jnp.concatenate([attn[o, :] for o in order], axis=0)
    for i, o in enumerate(order):
        xs[pl.ds(i * quarter, quarter), :] = x[o, :]
    block = x.shape[1]
    own = dp * 2 + sub
    for b in range(w.shape[1] // block):
        cols = pl.ds(b * block, block)
        terms = dot(a, w[:, cols])
        terms += jnp.where(own == b, xs[...].astype(F32), 0.0)
        away[:, cols] = terms[: 2 * quarter].astype(BF16)
        kept[:, cols] = terms[2 * quarter :]


def attend_project(place, q, x, w, keys, values):
    rows, width = q.shape
    half = rows // 2
    blocks = len(keys)
    return pl.pallas_call(
        functools.partial(attend_project_kernel, heads=width // HD, blocks=blocks),
        out_shape=(
            jax.ShapeDtypeStruct((half, w.shape[1]), BF16),
            jax.ShapeDtypeStruct((half, w.shape[1]), F32),
        ),
        in_specs=[SMEM] + [VMEM] * (3 + 2 * blocks),
        out_specs=(VMEM, VMEM),
        scratch_shapes=[pltpu.VMEM((rows, width), BF16), pltpu.VMEM(x.shape, BF16)],
        compiler_params=pltpu.CompilerParams(vmem_limit_bytes=32 * 2**20),
        cost_estimate=pl.CostEstimate(
            flops=2 * rows * width * (w.shape[1] + 2 * blocks * rows),
            bytes_accessed=2 * w.size + 6 * half * w.shape[1],
            transcendentals=rows * rows * blocks * width // HD,
        ),
    )(place, q, x, w, *keys, *values)


def local_kernel(place, g0, g1, embed, gain, *refs, pieces):
    bridge = refs[:4]
    whole = refs[4:6]
    parts = refs[6 : 6 + 4 * pieces]
    out, bw, hid = refs[6 + 4 * pieces :]
    dp, sub, grp = place[1], place[2], place[3]
    patches = g0.shape[0]
    bytes_ = g0.shape[1] // DSLICE
    rows = patches * bytes_
    depth = bridge[0].shape[0]
    blocks = [dp * 2 + sub, dp * 2 + 1 - sub, (1 - dp) * 2 + sub, (1 - dp) * 2 + 1 - sub]
    for b, ref in zip(blocks, bridge):
        bw[pl.ds(pl.multiple_of(b * depth, depth), depth), :] = ref[...]
    glob = (g0[...] + g1[...].astype(F32)).astype(BF16)
    stacked = jnp.concatenate(
        [glob[:, p * DSLICE : (p + 1) * DSLICE] for p in range(bytes_)], axis=0
    )
    to = lax.broadcasted_iota(jnp.int32, (rows, rows), 0)
    frm = lax.broadcasted_iota(jnp.int32, (rows, rows), 1)
    pick = ((to % bytes_) * patches + to // bytes_ == frm).astype(BF16)
    by_patch = dot(pick, stacked).astype(BF16)
    byte_in = embed[...].astype(F32) + dot(by_patch, bw[...])
    mean_square = jnp.mean(byte_in * byte_in, axis=1, keepdims=True)
    hid[...] = (byte_in * lax.rsqrt(mean_square + 1e-05) * gain[...]).astype(BF16)
    width = whole[0].shape[1]
    for b, ref in zip(blocks[:2], whole):
        out[:, pl.ds(pl.multiple_of(b * width, 128), width)] = dot(hid[...], ref[...]).astype(BF16)
    k = parts[0].shape[0]
    half = k * pieces
    for i, b in enumerate(blocks[2:]):
        total = None
        for j in range(2):
            first = (grp if j == 0 else 1 - grp) * half
            for n in range(pieces):
                ref = parts[(i * 2 + j) * pieces + n]
                lhs = hid[:, pl.ds(pl.multiple_of(first + n * k, k), k)]
                term = dot(lhs, ref[...])
                total = term if total is None else total + term
        out[:, pl.ds(pl.multiple_of(b * width, 128), width)] = total.astype(BF16)


def local(place, g0, g1, embed, gain, bridge, whole, parts):
    rows = embed.shape[0]
    width = 4 * whole[0].shape[1]
    pieces = len(parts) // 4
    return pl.pallas_call(
        functools.partial(local_kernel, pieces=pieces),
        out_shape=jax.ShapeDtypeStruct((rows, width), BF16),
        in_specs=[SMEM] + [VMEM] * (4 + 4 + 2 + len(parts)),
        out_specs=VMEM,
        scratch_shapes=[pltpu.VMEM((DSLICE, DL), BF16), pltpu.VMEM((rows, DL), BF16)],
        compiler_params=pltpu.CompilerParams(vmem_limit_bytes=40 * 2**20),
        cost_estimate=pl.CostEstimate(
            flops=2 * rows * DL * (width + DSLICE),
            bytes_accessed=2 * DL * width + 2 * rows * width,
            transcendentals=rows,
        ),
    )(place, g0, g1, embed, gain, *bridge, *whole, *parts)


def swap(x, axis):
    return lax.ppermute(x, axis, [(0, 1), (1, 0)])


def small_mesh(
    q_glob, k_glob, v_glob, x_glob, out_weight, bridge_weight, byte_embed, norm_gain, qkv_weight
):
    ctx_size = lax.axis_size("ctx")
    ctx, dp, sub, grp = (lax.axis_index(a) for a in ("ctx", "dp", "sub", "groups"))
    place = jnp.stack([ctx, dp, sub, grp]).astype(jnp.int32)
    keys, values = [k_glob], [v_glob]
    for s in range(1, ctx_size):
        hops = [(i, i + s) for i in range(ctx_size - s)]
        keys.append(lax.ppermute(k_glob, "ctx", hops))
        values.append(lax.ppermute(v_glob, "ctx", hops))

    pieces = 2
    depth = qkv_weight.shape[0] // 2 // pieces
    fetched = []
    for n in range(pieces):
        piece = lax.dynamic_slice_in_dim(qkv_weight, (grp * pieces + n) * depth, depth, 0)
        fetched.append(swap(piece, "dp"))
    passed = [swap(f, "groups") for f in fetched]
    core_fetched = [swap(f, "sub") for f in fetched]
    core_passed = [swap(f, "sub") for f in passed]
    other_core = swap(qkv_weight, "sub")
    bridge_chip = swap(bridge_weight, "dp")
    bridge = [bridge_weight, swap(bridge_weight, "sub"), bridge_chip, swap(bridge_chip, "sub")]

    away, kept = attend_project(place, q_glob, x_glob, out_weight, keys, values)
    summed = kept + swap(away, "sub").astype(F32)
    mid = summed.shape[0] // 2
    across = swap(summed[:mid].astype(BF16), "dp")
    rows = byte_embed.shape[0] * byte_embed.shape[1]
    result = local(
        place,
        summed[mid:],
        across,
        byte_embed.reshape(rows, DL),
        norm_gain.reshape(1, DL),
        bridge,
        [qkv_weight, other_core],
        fetched + passed + core_fetched + core_passed,
    )
    return result.reshape(byte_embed.shape[0], P_SIZE, result.shape[1])


def solution(mesh):
    rows = P(("groups", "ctx"), GROUP)
    in_specs = (
        rows,
        rows,
        rows,
        rows,
        P(GROUP, None),
        P(GROUP, None),
        P(("groups", "ctx", "dp", "sub"), None, None),
        P(),
        P(None, GROUP),
    )
    out_specs = P(("groups", "ctx", "dp", "sub"), None, None)
    pairs = all(mesh.shape[a] == 2 for a in ("groups", "dp", "sub"))
    per_device = small_mesh if pairs and mesh.shape["ctx"] <= 4 else any_mesh
    return jax.shard_map(
        per_device, mesh=mesh, in_specs=in_specs, out_specs=out_specs, check_vma=False
    )
```

```python
import functools
import math

import jax
import jax.numpy as jnp
from jax import lax
from jax.experimental import pallas as pl
from jax.experimental.pallas import tpu as pltpu
from jax.sharding import PartitionSpec as P

HD = 128
DL = 1024
P_SIZE = 8
DSLICE = 512
GROUP = ("dp", "sub")
SCALE = 1.0 / math.sqrt(HD)
VMEM = pl.BlockSpec(memory_space=pltpu.VMEM)
SMEM = pl.BlockSpec(memory_space=pltpu.SMEM)
F32 = jnp.float32
BF16 = jnp.bfloat16


def dot(a, b):
    return jnp.dot(a, b, preferred_element_type=F32)


def any_mesh(
    q_glob, k_glob, v_glob, x_glob, out_weight, bridge_weight, byte_embed, norm_gain, qkv_weight
):
    query_rows, query_width = q_glob.shape
    head_count = query_width // HD
    first_row = lax.axis_index("ctx") * query_rows
    queries = q_glob.reshape(query_rows, head_count, HD)
    query_pos = first_row + lax.iota(jnp.int32, query_rows)
    keys = lax.all_gather(k_glob, "ctx", axis=0, tiled=True)
    values = lax.all_gather(v_glob, "ctx", axis=0, tiled=True)
    count = keys.shape[0]
    keys = keys.reshape(count, head_count, HD)
    values = values.reshape(count, head_count, HD)
    scores = jnp.einsum("qhd,khd->hqk", queries, keys, preferred_element_type=F32) * SCALE
    allowed = query_pos[:, None] >= lax.iota(jnp.int32, count)[None, :]
    scores = jnp.where(allowed[None], scores, -jnp.inf)
    weights = jnp.exp(scores - jnp.max(scores, axis=2)[:, :, None])
    row_sum = jnp.sum(weights, axis=2)
    weighted = jnp.einsum("hqk,khd->hqd", weights.astype(BF16), values, preferred_element_type=F32)
    attn = (weighted / row_sum[:, :, None]).astype(BF16)
    attn = attn.transpose(1, 0, 2).reshape(query_rows, query_width)
    head_terms = dot(attn, out_weight)
    own_bytes = P_SIZE // lax.axis_size(GROUP)
    feature_sum = lax.psum_scatter(
        head_terms.astype(BF16), GROUP, scatter_dimension=1, tiled=True
    ).astype(F32)
    patch_out = (feature_sum + x_glob.astype(F32)).astype(BF16)
    patch_out = patch_out.reshape(query_rows, own_bytes, DSLICE)
    patch_out = lax.all_to_all(patch_out, GROUP, split_axis=0, concat_axis=1, tiled=True)
    glob_bytes = patch_out.reshape(-1, DSLICE)
    byte_rows = glob_bytes.shape[0]
    bridged = dot(glob_bytes, lax.all_gather(bridge_weight, GROUP, axis=0, tiled=True))
    byte_in = byte_embed.reshape(byte_rows, DL).astype(F32) + bridged
    mean_square = jnp.mean(byte_in * byte_in, axis=1, keepdims=True)
    normalized = (byte_in * lax.rsqrt(mean_square + 1e-05) * norm_gain).astype(BF16)
    result = dot(normalized, lax.all_gather(qkv_weight, GROUP, axis=1, tiled=True)).astype(BF16)
    return result.reshape(byte_embed.shape[0], P_SIZE, 3 * DL)


def attend_kernel(place, q, q_up, q_up2, k, v, k_low, v_low, own, own_log, up, up2):
    rows, width = q.shape
    heads = width // HD
    has_low = place[0] == 1
    row = lax.broadcasted_iota(jnp.int32, (rows, 2 * rows), 0)
    col = lax.broadcasted_iota(jnp.int32, (rows, 2 * rows), 1)
    is_low = col >= rows
    full = jnp.logical_or(col < rows, has_low)
    causal = jnp.logical_or(row >= col, jnp.logical_and(is_low, has_low))
    logs = [[], [], []]
    for h in range(heads):
        cols = pl.ds(h * HD, HD)
        kh = jnp.concatenate([k[:, cols], k_low[:, cols]], axis=0)
        vh = jnp.concatenate([v[:, cols], v_low[:, cols]], axis=0)
        for i, (queries, mask, target) in enumerate(
            ((q, causal, own), (q_up, full, up), (q_up2, full, up2))
        ):
            scores = lax.dot_general(
                queries[:, cols], kh, (((1,), (1,)), ((), ())), preferred_element_type=F32
            ) * SCALE
            scores = jnp.where(mask, scores, -jnp.inf)
            top = jnp.max(scores, axis=1, keepdims=True)
            probs = jnp.exp(scores - top)
            total = jnp.sum(probs, axis=1, keepdims=True)
            mixed = dot(probs.astype(BF16), vh) / total
            target[pl.ds(0, rows), cols] = mixed.astype(target.dtype)
            logs[i].append(top + jnp.log(total))
    lane = lax.broadcasted_iota(jnp.int32, (rows, HD), 1)

    def by_lane(columns):
        table = jnp.zeros((rows, HD), F32)
        for i, column in enumerate(columns):
            table = jnp.where(lane == i, column, table)
        return table

    own_log[...] = by_lane(logs[0])
    for target, log in ((up, logs[1]), (up2, logs[2])):
        terms = []
        rest = log
        for _ in range(3):
            high = [r.astype(BF16).astype(F32) for r in rest]
            rest = [r - t for r, t in zip(rest, high)]
            terms += high
        table = by_lane(terms).T
        target[pl.ds(rows, 16), :] = jnp.zeros((16, width), BF16)
        target[pl.ds(rows, 16), pl.ds(0, HD)] = table[:16, :rows].astype(BF16)


def attend(place, q, q_up, q_up2, k, v, k_low, v_low):
    rows, width = q.shape
    sent = jax.ShapeDtypeStruct((rows + 16, width), BF16)
    return pl.pallas_call(
        attend_kernel,
        out_shape=(
            jax.ShapeDtypeStruct((rows, width), F32),
            jax.ShapeDtypeStruct((rows, HD), F32),
            sent,
            sent,
        ),
        in_specs=[SMEM] + [VMEM] * 7,
        out_specs=(VMEM,) * 4,
        compiler_params=pltpu.CompilerParams(vmem_limit_bytes=16 * 2**20),
        cost_estimate=pl.CostEstimate(
            flops=24 * rows * rows * width,
            bytes_accessed=24 * rows * width,
            transcendentals=6 * rows * rows * width // HD,
        ),
    )(place, q, q_up, q_up2, k, v, k_low, v_low)


def project_kernel(place, own, own_log, low, low2, x, w, away, kept, attn, xs):
    ctx, dp, sub = place[0], place[1], place[2]
    rows, width = own.shape
    heads = width // HD
    quarter = rows // 4
    logs = [own_log[...]]
    for part in (low, low2):
        table = part[pl.ds(rows, 16), pl.ds(0, HD)].astype(F32)
        table = jnp.concatenate([table, jnp.zeros((HD - 16, HD), F32)], axis=0).T
        logs.append(table)
    valid = (ctx >= 2, ctx >= 3)
    for h in range(heads):
        cols = pl.ds(h * HD, HD)
        log = [logs[0][:, h : h + 1]]
        for table, ok in zip(logs[1:], valid):
            value = (
                table[:, h : h + 1]
                + table[:, heads + h : heads + h + 1]
                + table[:, 2 * heads + h : 2 * heads + h + 1]
            )
            log.append(jnp.where(ok, value, -jnp.inf))
        top = jnp.maximum(jnp.maximum(log[0], log[1]), log[2])
        share = [jnp.exp(value - top) for value in log]
        mixed = (
            share[0] * own[:, cols]
            + share[1] * low[pl.ds(0, rows), cols].astype(F32)
            + share[2] * low2[pl.ds(0, rows), cols].astype(F32)
        )
        attn[:, cols] = (mixed / (share[0] + share[1] + share[2])).astype(BF16)
    order = []
    for core in (1 - sub, sub):
        for chip in (1 - dp, dp):
            order.append(pl.ds(pl.multiple_of((chip * 2 + core) * quarter, quarter), quarter))
    a = jnp.concatenate([attn[o, :] for o in order], axis=0)
    for i, o in enumerate(order):
        xs[pl.ds(i * quarter, quarter), :] = x[o, :]
    block = x.shape[1]
    mine = dp * 2 + sub
    for b in range(w.shape[1] // block):
        cols = pl.ds(b * block, block)
        terms = dot(a, w[:, cols])
        terms += jnp.where(mine == b, xs[...].astype(F32), 0.0)
        away[:, cols] = terms[: 2 * quarter].astype(BF16)
        kept[:, cols] = terms[2 * quarter :]


def project(place, own, own_log, low, low2, x, w):
    rows, width = own.shape
    half = rows // 2
    return pl.pallas_call(
        project_kernel,
        out_shape=(
            jax.ShapeDtypeStruct((half, w.shape[1]), BF16),
            jax.ShapeDtypeStruct((half, w.shape[1]), F32),
        ),
        in_specs=[SMEM] + [VMEM] * 6,
        out_specs=(VMEM, VMEM),
        scratch_shapes=[pltpu.VMEM((rows, width), BF16), pltpu.VMEM(x.shape, BF16)],
        compiler_params=pltpu.CompilerParams(vmem_limit_bytes=24 * 2**20),
        cost_estimate=pl.CostEstimate(
            flops=2 * rows * width * w.shape[1],
            bytes_accessed=2 * w.size + 6 * half * w.shape[1],
            transcendentals=3 * rows * width // HD,
        ),
    )(place, own, own_log, low, low2, x, w)


def local_kernel(place, g0, g1, embed, gain, *refs, pieces):
    bridge = refs[:4]
    whole = refs[4:6]
    parts = refs[6 : 6 + 4 * pieces]
    out, bw, hid = refs[6 + 4 * pieces :]
    dp, sub, grp = place[1], place[2], place[3]
    patches = g0.shape[0]
    bytes_ = g0.shape[1] // DSLICE
    rows = patches * bytes_
    depth = bridge[0].shape[0]
    blocks = [dp * 2 + sub, dp * 2 + 1 - sub, (1 - dp) * 2 + sub, (1 - dp) * 2 + 1 - sub]
    for b, ref in zip(blocks, bridge):
        bw[pl.ds(pl.multiple_of(b * depth, depth), depth), :] = ref[...]
    glob = (g0[...] + g1[...].astype(F32)).astype(BF16)
    stacked = jnp.concatenate(
        [glob[:, p * DSLICE : (p + 1) * DSLICE] for p in range(bytes_)], axis=0
    )
    to = lax.broadcasted_iota(jnp.int32, (rows, rows), 0)
    frm = lax.broadcasted_iota(jnp.int32, (rows, rows), 1)
    pick = ((to % bytes_) * patches + to // bytes_ == frm).astype(BF16)
    by_patch = dot(pick, stacked).astype(BF16)
    byte_in = embed[...].astype(F32) + dot(by_patch, bw[...])
    mean_square = jnp.mean(byte_in * byte_in, axis=1, keepdims=True)
    hid[...] = (byte_in * lax.rsqrt(mean_square + 1e-05) * gain[...]).astype(BF16)
    width = whole[0].shape[1]
    for b, ref in zip(blocks[:2], whole):
        out[:, pl.ds(pl.multiple_of(b * width, 128), width)] = dot(hid[...], ref[...]).astype(BF16)
    k = parts[0].shape[0]
    half = k * pieces
    for i, b in enumerate(blocks[2:]):
        total = None
        for j in range(2):
            first = (grp if j == 0 else 1 - grp) * half
            for n in range(pieces):
                ref = parts[(i * 2 + j) * pieces + n]
                lhs = hid[:, pl.ds(pl.multiple_of(first + n * k, k), k)]
                term = dot(lhs, ref[...])
                total = term if total is None else total + term
        out[:, pl.ds(pl.multiple_of(b * width, 128), width)] = total.astype(BF16)


def local(place, g0, g1, embed, gain, bridge, whole, parts):
    rows = embed.shape[0]
    width = 4 * whole[0].shape[1]
    pieces = len(parts) // 4
    return pl.pallas_call(
        functools.partial(local_kernel, pieces=pieces),
        out_shape=jax.ShapeDtypeStruct((rows, width), BF16),
        in_specs=[SMEM] + [VMEM] * (4 + 4 + 2 + len(parts)),
        out_specs=VMEM,
        scratch_shapes=[pltpu.VMEM((DSLICE, DL), BF16), pltpu.VMEM((rows, DL), BF16)],
        compiler_params=pltpu.CompilerParams(vmem_limit_bytes=40 * 2**20),
        cost_estimate=pl.CostEstimate(
            flops=2 * rows * DL * (width + DSLICE),
            bytes_accessed=2 * DL * width + 2 * rows * width,
            transcendentals=rows,
        ),
    )(place, g0, g1, embed, gain, *bridge, *whole, *parts)


def swap(x, axis):
    return lax.ppermute(x, axis, [(0, 1), (1, 0)])


def small_mesh(
    q_glob, k_glob, v_glob, x_glob, out_weight, bridge_weight, byte_embed, norm_gain, qkv_weight
):
    ctx, dp, sub, grp = (lax.axis_index(a) for a in ("ctx", "dp", "sub", "groups"))
    place = jnp.stack([ctx, dp, sub, grp]).astype(jnp.int32)
    pieces = 2
    depth = qkv_weight.shape[0] // 2 // pieces
    own_pieces = [
        lax.dynamic_slice_in_dim(qkv_weight, (grp * pieces + n) * depth, depth, 0)
        for n in range(pieces)
    ]

    fetched = [swap(own_pieces[0], "dp")]
    bridge_chip = swap(bridge_weight, "dp")
    bridge_core = swap(bridge_weight, "sub")
    other_core = swap(qkv_weight, "sub")
    k_low = lax.ppermute(k_glob, "ctx", [(0, 1)])
    v_low = lax.ppermute(v_glob, "ctx", [(0, 1)])
    q_up = lax.ppermute(q_glob, "ctx", [(2, 1), (3, 2)])
    q_up2 = lax.ppermute(q_glob, "ctx", [(3, 1)])
    (k_low, v_low, q_up, q_up2, fetched[0], bridge_chip, piece) = lax.optimization_barrier(
        (k_low, v_low, q_up, q_up2, fetched[0], bridge_chip, own_pieces[1])
    )

    fetched.append(swap(piece, "dp"))
    passed = [swap(fetched[0], "groups")]
    core_fetched = [swap(fetched[0], "sub")]
    bridge_both = swap(bridge_chip, "sub")
    own, own_log, up, up2 = attend(place, q_glob, q_up, q_up2, k_glob, v_glob, k_low, v_low)
    low = lax.ppermute(up, "ctx", [(1, 2), (2, 3)])
    low2 = lax.ppermute(up2, "ctx", [(1, 3)])
    (low, low2, fetched[1], passed[0]) = lax.optimization_barrier(
        (low, low2, fetched[1], passed[0])
    )

    passed.append(swap(fetched[1], "groups"))
    core_fetched.append(swap(fetched[1], "sub"))
    core_passed = [swap(p, "sub") for p in passed]
    away, kept = project(place, own, own_log, low, low2, x_glob, out_weight)
    summed = kept + swap(away, "sub").astype(F32)
    mid = summed.shape[0] // 2
    across = swap(summed[:mid].astype(BF16), "dp")
    rows = byte_embed.shape[0] * byte_embed.shape[1]
    result = local(
        place,
        summed[mid:],
        across,
        byte_embed.reshape(rows, DL),
        norm_gain.reshape(1, DL),
        [bridge_weight, bridge_core, bridge_chip, bridge_both],
        [qkv_weight, other_core],
        fetched + passed + core_fetched + core_passed,
    )
    return result.reshape(byte_embed.shape[0], P_SIZE, result.shape[1])


def solution(mesh):
    rows = P(("groups", "ctx"), GROUP)
    in_specs = (
        rows,
        rows,
        rows,
        rows,
        P(GROUP, None),
        P(GROUP, None),
        P(("groups", "ctx", "dp", "sub"), None, None),
        P(),
        P(None, GROUP),
    )
    out_specs = P(("groups", "ctx", "dp", "sub"), None, None)
    pairs = all(mesh.shape[a] == 2 for a in ("groups", "dp", "sub"))
    per_device = small_mesh if pairs and mesh.shape["ctx"] == 4 else any_mesh
    return jax.shard_map(
        per_device, mesh=mesh, in_specs=in_specs, out_specs=out_specs, check_vma=False
    )
```

```python
import functools
import math

import jax
import jax.numpy as jnp
from jax import lax
from jax.experimental import pallas as pl
from jax.experimental.pallas import tpu as pltpu
from jax.sharding import PartitionSpec as P

HD = 128
DL = 1024
P_SIZE = 8
DSLICE = 512
GROUP = ("dp", "sub")
SCALE = 1.0 / math.sqrt(HD)
VMEM = pl.BlockSpec(memory_space=pltpu.VMEM)
SMEM = pl.BlockSpec(memory_space=pltpu.SMEM)
HBM = pl.BlockSpec(memory_space=pltpu.HBM)
F32 = jnp.float32
BF16 = jnp.bfloat16


def dot(a, b):
    return jnp.dot(a, b, preferred_element_type=F32)


def any_mesh(
    q_glob, k_glob, v_glob, x_glob, out_weight, bridge_weight, byte_embed, norm_gain, qkv_weight
):
    query_rows, query_width = q_glob.shape
    head_count = query_width // HD
    first_row = lax.axis_index("ctx") * query_rows
    queries = q_glob.reshape(query_rows, head_count, HD)
    query_pos = first_row + lax.iota(jnp.int32, query_rows)
    keys = lax.all_gather(k_glob, "ctx", axis=0, tiled=True)
    values = lax.all_gather(v_glob, "ctx", axis=0, tiled=True)
    count = keys.shape[0]
    keys = keys.reshape(count, head_count, HD)
    values = values.reshape(count, head_count, HD)
    scores = jnp.einsum("qhd,khd->hqk", queries, keys, preferred_element_type=F32) * SCALE
    allowed = query_pos[:, None] >= lax.iota(jnp.int32, count)[None, :]
    scores = jnp.where(allowed[None], scores, -jnp.inf)
    weights = jnp.exp(scores - jnp.max(scores, axis=2)[:, :, None])
    row_sum = jnp.sum(weights, axis=2)
    weighted = jnp.einsum("hqk,khd->hqd", weights.astype(BF16), values, preferred_element_type=F32)
    attn = (weighted / row_sum[:, :, None]).astype(BF16)
    attn = attn.transpose(1, 0, 2).reshape(query_rows, query_width)
    head_terms = dot(attn, out_weight)
    own_bytes = P_SIZE // lax.axis_size(GROUP)
    feature_sum = lax.psum_scatter(
        head_terms.astype(BF16), GROUP, scatter_dimension=1, tiled=True
    ).astype(F32)
    patch_out = (feature_sum + x_glob.astype(F32)).astype(BF16)
    patch_out = patch_out.reshape(query_rows, own_bytes, DSLICE)
    patch_out = lax.all_to_all(patch_out, GROUP, split_axis=0, concat_axis=1, tiled=True)
    glob_bytes = patch_out.reshape(-1, DSLICE)
    byte_rows = glob_bytes.shape[0]
    bridged = dot(glob_bytes, lax.all_gather(bridge_weight, GROUP, axis=0, tiled=True))
    byte_in = byte_embed.reshape(byte_rows, DL).astype(F32) + bridged
    mean_square = jnp.mean(byte_in * byte_in, axis=1, keepdims=True)
    normalized = (byte_in * lax.rsqrt(mean_square + 1e-05) * norm_gain).astype(BF16)
    result = dot(normalized, lax.all_gather(qkv_weight, GROUP, axis=1, tiled=True)).astype(BF16)
    return result.reshape(byte_embed.shape[0], P_SIZE, 3 * DL)


def attend_kernel(place, held, q_up, k_low, v_low, own, own_log, up):
    rows, width = q_up.shape
    heads = width // HD
    has_low = place[0] >= 1
    row = lax.broadcasted_iota(jnp.int32, (rows, 2 * rows), 0)
    col = lax.broadcasted_iota(jnp.int32, (rows, 2 * rows), 1)
    low = jnp.logical_and(col >= rows, has_low)
    full = jnp.logical_or(col < rows, low)
    causal = jnp.logical_or(row >= col, low)
    logs = [[], []]
    for h in range(heads):
        cols = pl.ds(h * HD, HD)
        qh, k, v = (held[:, pl.ds(i * width + h * HD, HD)] for i in range(3))
        kh = jnp.concatenate([k, k_low[:, cols]], axis=0)
        vh = jnp.concatenate([v, v_low[:, cols]], axis=0)
        for i, (queries, mask, target) in enumerate(((qh, causal, own), (q_up[:, cols], full, up))):
            scores = lax.dot_general(
                queries, kh, (((1,), (1,)), ((), ())), preferred_element_type=F32
            ) * SCALE
            scores = jnp.where(mask, scores, -jnp.inf)
            top = jnp.max(scores, axis=1, keepdims=True)
            probs = jnp.exp(scores - top)
            total = jnp.sum(probs, axis=1, keepdims=True)
            mixed = dot(probs.astype(BF16), vh) / total
            target[pl.ds(0, rows), cols] = mixed.astype(target.dtype)
            logs[i].append(top + jnp.log(total))
    lane = lax.broadcasted_iota(jnp.int32, (rows, HD), 1)

    def by_lane(columns):
        table = jnp.zeros((rows, HD), F32)
        for i, column in enumerate(columns):
            table = jnp.where(lane == i, column, table)
        return table

    own_log[...] = by_lane(logs[0])
    terms = []
    rest = logs[1]
    for _ in range(3):
        high = [r.astype(BF16).astype(F32) for r in rest]
        rest = [r - t for r, t in zip(rest, high)]
        terms += high
    up[pl.ds(rows, 16), :] = jnp.zeros((16, width), BF16)
    up[pl.ds(rows, 16), pl.ds(0, HD)] = by_lane(terms).T[:16, :rows].astype(BF16)


def attend(place, held, q_up, k_low, v_low):
    rows, width = q_up.shape
    return pl.pallas_call(
        attend_kernel,
        out_shape=(
            jax.ShapeDtypeStruct((rows, width), F32),
            jax.ShapeDtypeStruct((rows, HD), F32),
            jax.ShapeDtypeStruct((rows + 16, width), BF16),
        ),
        in_specs=[SMEM] + [VMEM] * 4,
        out_specs=(VMEM,) * 3,
        compiler_params=pltpu.CompilerParams(vmem_limit_bytes=6 * 2**20),
        cost_estimate=pl.CostEstimate(
            flops=16 * rows * rows * width,
            bytes_accessed=24 * rows * width,
            transcendentals=4 * rows * rows * width // HD,
        ),
    )(place, held, q_up, k_low, v_low)


def copy_all(pairs, sems):
    copies = [pltpu.make_async_copy(a, b, sems.at[i]) for i, (a, b) in enumerate(pairs)]
    for copy in copies:
        copy.start()
    for copy in copies:
        copy.wait()


def hold_kernel(q, k, v, held):
    width = q.shape[1]
    for i, source in enumerate((q, k, v)):
        held[:, pl.ds(i * width, width)] = source[...]


def hold(q, k, v):
    return pl.pallas_call(
        hold_kernel,
        out_shape=jax.ShapeDtypeStruct((q.shape[0], 3 * q.shape[1]), q.dtype),
        in_specs=[VMEM] * 3,
        out_specs=VMEM,
        compiler_params=pltpu.CompilerParams(vmem_limit_bytes=2 * 2**20),
    )(q, k, v)


def bring_kernel(source, target, sems):
    rows = source.shape[0] // sems.shape[0]
    cuts = [pl.ds(i * rows, rows) for i in range(sems.shape[0])]
    copy_all([(source.at[c, :], target.at[c, :]) for c in cuts], sems)


def bring(x, parts):
    return pl.pallas_call(
        bring_kernel,
        out_shape=jax.ShapeDtypeStruct(x.shape, x.dtype),
        in_specs=[HBM],
        out_specs=VMEM,
        scratch_shapes=[pltpu.SemaphoreType.DMA((parts,))],
        compiler_params=pltpu.CompilerParams(vmem_limit_bytes=2 * 2**20),
    )(x)


def project_kernel(place, own, own_log, low, x, w, away, kept, attn, xs):
    ctx, dp, sub = place[0], place[1], place[2]
    rows, width = own.shape
    heads = width // HD
    quarter = rows // 4
    table = low[pl.ds(rows, 16), pl.ds(0, HD)].astype(F32)
    table = jnp.concatenate([table, jnp.zeros((HD - 16, HD), F32)], axis=0).T
    for h in range(heads):
        cols = pl.ds(h * HD, HD)
        log = own_log[:, h : h + 1]
        log_low = (
            table[:, h : h + 1]
            + table[:, heads + h : heads + h + 1]
            + table[:, 2 * heads + h : 2 * heads + h + 1]
        )
        log_low = jnp.where(ctx >= 2, log_low, -jnp.inf)
        top = jnp.maximum(log, log_low)
        share, share_low = jnp.exp(log - top), jnp.exp(log_low - top)
        mixed = share * own[:, cols] + share_low * low[pl.ds(0, rows), cols].astype(F32)
        attn[:, cols] = (mixed / (share + share_low)).astype(BF16)
    order = []
    for core in (1 - sub, sub):
        for chip in (1 - dp, dp):
            order.append(pl.ds(pl.multiple_of((chip * 2 + core) * quarter, quarter), quarter))
    a = jnp.concatenate([attn[o, :] for o in order], axis=0)
    for i, o in enumerate(order):
        xs[pl.ds(i * quarter, quarter), :] = x[o, :]
    block = x.shape[1]
    mine = dp * 2 + sub
    for b in range(w.shape[1] // block):
        cols = pl.ds(b * block, block)
        terms = dot(a, w[:, cols])
        terms += jnp.where(mine == b, xs[...].astype(F32), 0.0)
        away[:, cols] = terms[: 2 * quarter].astype(BF16)
        kept[:, cols] = terms[2 * quarter :]


def project(place, own, own_log, low, x, w):
    rows, width = own.shape
    half = rows // 2
    return pl.pallas_call(
        project_kernel,
        out_shape=(
            jax.ShapeDtypeStruct((half, w.shape[1]), BF16),
            jax.ShapeDtypeStruct((half, w.shape[1]), F32),
        ),
        in_specs=[SMEM] + [VMEM] * 5,
        out_specs=(VMEM, VMEM),
        scratch_shapes=[pltpu.VMEM((rows, width), BF16), pltpu.VMEM(x.shape, BF16)],
        compiler_params=pltpu.CompilerParams(vmem_limit_bytes=12 * 2**20),
        cost_estimate=pl.CostEstimate(
            flops=2 * rows * width * w.shape[1],
            bytes_accessed=2 * w.size + 6 * half * w.shape[1],
            transcendentals=3 * rows * width // HD,
        ),
    )(place, own, own_log, low, x, w)


def bytes_kernel(place, g0, g1, embed, gain, *refs):
    bridge = refs[:4]
    hid, bw = refs[4:]
    dp, sub = place[1], place[2]
    patches = g0.shape[0]
    bytes_ = g0.shape[1] // DSLICE
    rows = patches * bytes_
    depth = bridge[0].shape[0]
    for b, ref in zip(block_order(dp, sub), bridge):
        bw[pl.ds(pl.multiple_of(b * depth, depth), depth), :] = ref[...]
    glob = (g0[...] + g1[...].astype(F32)).astype(BF16)
    stacked = jnp.concatenate(
        [glob[:, p * DSLICE : (p + 1) * DSLICE] for p in range(bytes_)], axis=0
    )
    to = lax.broadcasted_iota(jnp.int32, (rows, rows), 0)
    source = lax.broadcasted_iota(jnp.int32, (rows, rows), 1)
    pick = ((to % bytes_) * patches + to // bytes_ == source).astype(BF16)
    by_patch = dot(pick, stacked).astype(BF16)
    byte_in = embed[...].astype(F32) + dot(by_patch, bw[...])
    mean_square = jnp.mean(byte_in * byte_in, axis=1, keepdims=True)
    hid[...] = (byte_in * lax.rsqrt(mean_square + 1e-05) * gain[...]).astype(BF16)


def block_order(dp, sub):
    return [dp * 2 + sub, dp * 2 + 1 - sub, (1 - dp) * 2 + sub, (1 - dp) * 2 + 1 - sub]


def bytes_in(place, g0, g1, embed, gain, bridge):
    rows = embed.shape[0]
    return pl.pallas_call(
        bytes_kernel,
        out_shape=jax.ShapeDtypeStruct((rows, DL), BF16),
        in_specs=[SMEM] + [VMEM] * 8,
        out_specs=VMEM,
        scratch_shapes=[pltpu.VMEM((DSLICE, DL), BF16)],
        compiler_params=pltpu.CompilerParams(vmem_limit_bytes=10 * 2**20),
        cost_estimate=pl.CostEstimate(
            flops=2 * rows * DL * DSLICE, bytes_accessed=6 * rows * DL, transcendentals=rows
        ),
    )(place, g0, g1, embed, gain, *bridge)


def local_kernel(place, hid, *refs):
    whole, chips = refs[:2], (refs[2:7], refs[7:12])
    out, held, sems = refs[12:]
    ctx, dp, sub, grp = (place[i] for i in range(4))
    odd = ctx % 2
    depth, width = whole[0].shape
    quarter, eighth = depth // 4, depth // 8

    def columns(first, count):
        return hid[:, pl.ds(pl.multiple_of(first, 128), count)]

    copies = []
    for i, b in enumerate(block_order(dp, sub)):
        if i < 2:
            total = dot(hid[...], whole[i][...])
        else:
            x0, y0, x1, y1, z1 = chips[i - 2]
            total = dot(columns(grp * quarter, quarter), x0[...])
            total += dot(columns((1 - grp) * quarter, quarter), y0[...])
            mixed = [columns(4 * eighth + grp * eighth, eighth), columns(6 * eighth + odd * eighth, eighth)]
            total += dot(jnp.concatenate(mixed, axis=1), x1[...])
            total += dot(columns(4 * eighth + (1 - grp) * eighth, eighth), y1[...])
            total += dot(columns(6 * eighth + (1 - odd) * eighth, eighth), z1[...])
        held[i, :, :] = total.astype(BF16)
        copy = pltpu.make_async_copy(
            held.at[i], out.at[:, pl.ds(pl.multiple_of(b * width, 128), width)], sems.at[i]
        )
        copy.start()
        copies.append(copy)
    for copy in copies:
        copy.wait()


def local(place, hid, *weights):
    rows = hid.shape[0]
    block = weights[0].shape[1]
    return pl.pallas_call(
        local_kernel,
        out_shape=jax.ShapeDtypeStruct((rows, 4 * block), BF16),
        in_specs=[SMEM] + [VMEM] * (1 + len(weights)),
        out_specs=pl.BlockSpec(memory_space=pl.ANY),
        scratch_shapes=[pltpu.VMEM((4, rows, block), BF16), pltpu.SemaphoreType.DMA((4,))],
        compiler_params=pltpu.CompilerParams(vmem_limit_bytes=12 * 2**20),
        cost_estimate=pl.CostEstimate(
            flops=8 * rows * DL * block,
            bytes_accessed=8 * DL * block + 8 * rows * block,
            transcendentals=0,
        ),
    )(place, hid, *weights)


def swap(x, axis):
    return lax.ppermute(x, axis, [(0, 1), (1, 0)])


def after(x, *events):
    return lax.optimization_barrier((x, *events))[0]


def small_mesh(
    q_glob, k_glob, v_glob, x_glob, out_weight, bridge_weight, byte_embed, norm_gain, qkv_weight
):
    ctx, dp, sub, grp = (lax.axis_index(a) for a in ("ctx", "dp", "sub", "groups"))
    place = jnp.stack([ctx, dp, sub, grp]).astype(jnp.int32)

    quarter, eighth = qkv_weight.shape[0] // 4, qkv_weight.shape[0] // 8
    held = hold(q_glob, k_glob, v_glob)
    later = after(qkv_weight, held)
    w0 = lax.dynamic_slice_in_dim(qkv_weight, grp * quarter, quarter, 0)
    w1 = jnp.concatenate(
        [
            lax.dynamic_slice_in_dim(later, (4 + grp) * eighth, eighth, 0),
            lax.dynamic_slice_in_dim(later, (6 + ctx % 2) * eighth, eighth, 0),
        ],
        axis=0,
    )

    x0 = swap(w0, "dp")
    bridge_x = swap(bridge_weight, "dp")
    q_up = lax.ppermute(q_glob, "ctx", [(2, 0), (3, 1)])
    k_low = lax.ppermute(k_glob, "ctx", [(0, 1), (1, 2), (2, 3)])
    v_low = lax.ppermute(v_glob, "ctx", [(0, 1), (1, 2), (2, 3)])
    q_up, k_low, v_low, x0, bridge_x, w1, held, bridge_weight, place = lax.optimization_barrier(
        (q_up, k_low, v_low, x0, bridge_x, w1, held, bridge_weight, place)
    )

    own, own_log, up = attend(place, held, q_up, k_low, v_low)
    low = lax.ppermute(up, "ctx", [(0, 2), (1, 3)])
    x1 = swap(w1, "dp")
    y0 = swap(x0, "groups")
    core_x0 = swap(x0, "sub")
    bridge_core = swap(bridge_weight, "sub")
    out_weight = bring(after(out_weight, up), 4)
    low, core_x0, x1, y0, out_weight, bridge_x, bridge_core, qkv_weight = lax.optimization_barrier(
        (low, core_x0, x1, y0, out_weight, bridge_x, bridge_core, qkv_weight)
    )

    away, kept = project(place, own, own_log, low, x_glob, out_weight)
    away = swap(away, "sub")
    core_y0 = swap(y0, "sub")
    bridge_both = swap(bridge_x, "sub")
    away, bridge_both, core_y0, x1, qkv_weight = lax.optimization_barrier(
        (away, bridge_both, core_y0, x1, qkv_weight)
    )

    summed = kept + away.astype(F32)
    mid = summed.shape[0] // 2
    across = swap(summed[:mid].astype(BF16), "dp")
    y1 = swap(x1[:eighth], "groups")
    z1 = lax.ppermute(x1[eighth:], "ctx", [(0, 1), (1, 0), (2, 3), (3, 2)])
    core_x1 = swap(x1, "sub")
    other_core = swap(qkv_weight, "sub")
    across, y1, z1, core_x1, other_core = lax.optimization_barrier(
        (across, y1, z1, core_x1, other_core)
    )

    core_y1 = swap(y1, "sub")
    core_z1 = swap(z1, "sub")
    rows = byte_embed.shape[0] * byte_embed.shape[1]
    hidden = bytes_in(
        place,
        summed[mid:],
        across,
        byte_embed.reshape(rows, DL),
        norm_gain.reshape(1, DL),
        [bridge_weight, bridge_core, bridge_x, bridge_both],
    )
    result = local(
        place,
        hidden,
        *(qkv_weight, other_core),
        *(x0, y0, x1, y1, z1),
        *(core_x0, core_y0, core_x1, core_y1, core_z1),
    )
    return result.reshape(byte_embed.shape[0], P_SIZE, result.shape[1])


def solution(mesh):
    rows = P(("groups", "ctx"), GROUP)
    in_specs = (
        rows,
        rows,
        rows,
        rows,
        P(GROUP, None),
        P(GROUP, None),
        P(("groups", "ctx", "dp", "sub"), None, None),
        P(),
        P(None, GROUP),
    )
    out_specs = P(("groups", "ctx", "dp", "sub"), None, None)
    pairs = all(mesh.shape[a] == 2 for a in ("groups", "dp", "sub"))
    per_device = small_mesh if pairs and mesh.shape["ctx"] == 4 else any_mesh
    return jax.shard_map(
        per_device, mesh=mesh, in_specs=in_specs, out_specs=out_specs, check_vma=False
    )
```

```python
import functools
import math

import jax
import jax.numpy as jnp
from jax import lax
from jax.experimental import pallas as pl
from jax.experimental.pallas import tpu as pltpu
from jax.sharding import PartitionSpec as P

HD = 128
DL = 1024
P_SIZE = 8
DSLICE = 512
GROUP = ("dp", "sub")
SCALE = 1.0 / math.sqrt(HD)
VMEM = pl.BlockSpec(memory_space=pltpu.VMEM)
SMEM = pl.BlockSpec(memory_space=pltpu.SMEM)
HBM = pl.BlockSpec(memory_space=pltpu.HBM)
F32 = jnp.float32
BF16 = jnp.bfloat16


def dot(a, b):
    return jnp.dot(a, b, preferred_element_type=F32)


def any_mesh(
    q_glob, k_glob, v_glob, x_glob, out_weight, bridge_weight, byte_embed, norm_gain, qkv_weight
):
    query_rows, query_width = q_glob.shape
    head_count = query_width // HD
    first_row = lax.axis_index("ctx") * query_rows
    queries = q_glob.reshape(query_rows, head_count, HD)
    query_pos = first_row + lax.iota(jnp.int32, query_rows)
    keys = lax.all_gather(k_glob, "ctx", axis=0, tiled=True)
    values = lax.all_gather(v_glob, "ctx", axis=0, tiled=True)
    count = keys.shape[0]
    keys = keys.reshape(count, head_count, HD)
    values = values.reshape(count, head_count, HD)
    scores = jnp.einsum("qhd,khd->hqk", queries, keys, preferred_element_type=F32) * SCALE
    allowed = query_pos[:, None] >= lax.iota(jnp.int32, count)[None, :]
    scores = jnp.where(allowed[None], scores, -jnp.inf)
    weights = jnp.exp(scores - jnp.max(scores, axis=2)[:, :, None])
    row_sum = jnp.sum(weights, axis=2)
    weighted = jnp.einsum("hqk,khd->hqd", weights.astype(BF16), values, preferred_element_type=F32)
    attn = (weighted / row_sum[:, :, None]).astype(BF16)
    attn = attn.transpose(1, 0, 2).reshape(query_rows, query_width)
    head_terms = dot(attn, out_weight)
    own_bytes = P_SIZE // lax.axis_size(GROUP)
    feature_sum = lax.psum_scatter(
        head_terms.astype(BF16), GROUP, scatter_dimension=1, tiled=True
    ).astype(F32)
    patch_out = (feature_sum + x_glob.astype(F32)).astype(BF16)
    patch_out = patch_out.reshape(query_rows, own_bytes, DSLICE)
    patch_out = lax.all_to_all(patch_out, GROUP, split_axis=0, concat_axis=1, tiled=True)
    glob_bytes = patch_out.reshape(-1, DSLICE)
    byte_rows = glob_bytes.shape[0]
    bridged = dot(glob_bytes, lax.all_gather(bridge_weight, GROUP, axis=0, tiled=True))
    byte_in = byte_embed.reshape(byte_rows, DL).astype(F32) + bridged
    mean_square = jnp.mean(byte_in * byte_in, axis=1, keepdims=True)
    normalized = (byte_in * lax.rsqrt(mean_square + 1e-05) * norm_gain).astype(BF16)
    result = dot(normalized, lax.all_gather(qkv_weight, GROUP, axis=1, tiled=True)).astype(BF16)
    return result.reshape(byte_embed.shape[0], P_SIZE, 3 * DL)


def attend_kernel(place, held, q_up, k_low, v_low, own, own_log, up):
    rows, width = q_up.shape
    heads = width // HD
    has_low = place[0] >= 1
    row = lax.broadcasted_iota(jnp.int32, (rows, 2 * rows), 0)
    col = lax.broadcasted_iota(jnp.int32, (rows, 2 * rows), 1)
    low = jnp.logical_and(col >= rows, has_low)
    full = jnp.logical_or(col < rows, low)
    causal = jnp.logical_or(row >= col, low)
    logs = [[], []]
    for h in range(heads):
        cols = pl.ds(h * HD, HD)
        qh, k, v = (held[:, pl.ds(i * width + h * HD, HD)] for i in range(3))
        kh = jnp.concatenate([k, k_low[:, cols]], axis=0)
        vh = jnp.concatenate([v, v_low[:, cols]], axis=0)
        for i, (queries, mask, target) in enumerate(((qh, causal, own), (q_up[:, cols], full, up))):
            scores = lax.dot_general(
                queries, kh, (((1,), (1,)), ((), ())), preferred_element_type=F32
            ) * SCALE
            scores = jnp.where(mask, scores, -jnp.inf)
            top = jnp.max(scores, axis=1, keepdims=True)
            probs = jnp.exp(scores - top)
            total = jnp.sum(probs, axis=1, keepdims=True)
            mixed = dot(probs.astype(BF16), vh) / total
            target[pl.ds(0, rows), cols] = mixed.astype(target.dtype)
            logs[i].append(top + jnp.log(total))
    lane = lax.broadcasted_iota(jnp.int32, (rows, HD), 1)

    def by_lane(columns):
        table = jnp.zeros((rows, HD), F32)
        for i, column in enumerate(columns):
            table = jnp.where(lane == i, column, table)
        return table

    own_log[...] = by_lane(logs[0])
    terms = []
    rest = logs[1]
    for _ in range(3):
        high = [r.astype(BF16).astype(F32) for r in rest]
        rest = [r - t for r, t in zip(rest, high)]
        terms += high
    up[pl.ds(rows, 16), :] = jnp.zeros((16, width), BF16)
    up[pl.ds(rows, 16), pl.ds(0, HD)] = by_lane(terms).T[:16, :rows].astype(BF16)


def attend(place, held, q_up, k_low, v_low):
    rows, width = q_up.shape
    return pl.pallas_call(
        attend_kernel,
        out_shape=(
            jax.ShapeDtypeStruct((rows, width), F32),
            jax.ShapeDtypeStruct((rows, HD), F32),
            jax.ShapeDtypeStruct((rows + 16, width), BF16),
        ),
        in_specs=[SMEM] + [VMEM] * 4,
        out_specs=(VMEM,) * 3,
        compiler_params=pltpu.CompilerParams(vmem_limit_bytes=6 * 2**20),
        cost_estimate=pl.CostEstimate(
            flops=16 * rows * rows * width,
            bytes_accessed=24 * rows * width,
            transcendentals=4 * rows * rows * width // HD,
        ),
    )(place, held, q_up, k_low, v_low)


def copy_all(pairs, sems):
    copies = [pltpu.make_async_copy(a, b, sems.at[i]) for i, (a, b) in enumerate(pairs)]
    for copy in copies:
        copy.start()
    for copy in copies:
        copy.wait()


def hold_kernel(q, k, v, held):
    width = q.shape[1]
    for i, source in enumerate((q, k, v)):
        held[:, pl.ds(i * width, width)] = source[...]


def hold(q, k, v):
    return pl.pallas_call(
        hold_kernel,
        out_shape=jax.ShapeDtypeStruct((q.shape[0], 3 * q.shape[1]), q.dtype),
        in_specs=[VMEM] * 3,
        out_specs=VMEM,
        compiler_params=pltpu.CompilerParams(vmem_limit_bytes=2 * 2**20),
    )(q, k, v)


def bring_kernel(source, target, sems):
    rows = source.shape[0] // sems.shape[0]
    cuts = [pl.ds(i * rows, rows) for i in range(sems.shape[0])]
    copy_all([(source.at[c, :], target.at[c, :]) for c in cuts], sems)


def bring(x, parts):
    return pl.pallas_call(
        bring_kernel,
        out_shape=jax.ShapeDtypeStruct(x.shape, x.dtype),
        in_specs=[HBM],
        out_specs=VMEM,
        scratch_shapes=[pltpu.SemaphoreType.DMA((parts,))],
        compiler_params=pltpu.CompilerParams(vmem_limit_bytes=2 * 2**20),
    )(x)


def project_kernel(place, own, own_log, low, x, w, away, kept, attn, xs):
    ctx, dp, sub = place[0], place[1], place[2]
    rows, width = own.shape
    heads = width // HD
    quarter = rows // 4
    table = low[pl.ds(rows, 16), pl.ds(0, HD)].astype(F32)
    table = jnp.concatenate([table, jnp.zeros((HD - 16, HD), F32)], axis=0).T
    for h in range(heads):
        cols = pl.ds(h * HD, HD)
        log = own_log[:, h : h + 1]
        log_low = (
            table[:, h : h + 1]
            + table[:, heads + h : heads + h + 1]
            + table[:, 2 * heads + h : 2 * heads + h + 1]
        )
        log_low = jnp.where(ctx >= 2, log_low, -jnp.inf)
        top = jnp.maximum(log, log_low)
        share, share_low = jnp.exp(log - top), jnp.exp(log_low - top)
        mixed = share * own[:, cols] + share_low * low[pl.ds(0, rows), cols].astype(F32)
        attn[:, cols] = (mixed / (share + share_low)).astype(BF16)
    order = []
    for core in (1 - sub, sub):
        for chip in (1 - dp, dp):
            order.append(pl.ds(pl.multiple_of((chip * 2 + core) * quarter, quarter), quarter))
    a = jnp.concatenate([attn[o, :] for o in order], axis=0)
    for i, o in enumerate(order):
        xs[pl.ds(i * quarter, quarter), :] = x[o, :]
    block = x.shape[1]
    mine = dp * 2 + sub
    for b in range(w.shape[1] // block):
        cols = pl.ds(b * block, block)
        terms = dot(a, w[:, cols])
        terms += jnp.where(mine == b, xs[...].astype(F32), 0.0)
        away[:, cols] = terms[: 2 * quarter].astype(BF16)
        kept[:, cols] = terms[2 * quarter :]


def project(place, own, own_log, low, x, w):
    rows, width = own.shape
    half = rows // 2
    return pl.pallas_call(
        project_kernel,
        out_shape=(
            jax.ShapeDtypeStruct((half, w.shape[1]), BF16),
            jax.ShapeDtypeStruct((half, w.shape[1]), F32),
        ),
        in_specs=[SMEM] + [VMEM] * 5,
        out_specs=(VMEM, VMEM),
        scratch_shapes=[pltpu.VMEM((rows, width), BF16), pltpu.VMEM(x.shape, BF16)],
        compiler_params=pltpu.CompilerParams(vmem_limit_bytes=12 * 2**20),
        cost_estimate=pl.CostEstimate(
            flops=2 * rows * width * w.shape[1],
            bytes_accessed=2 * w.size + 6 * half * w.shape[1],
            transcendentals=3 * rows * width // HD,
        ),
    )(place, own, own_log, low, x, w)


def bytes_kernel(place, g0, g1, embed, gain, *refs):
    bridge = refs[:4]
    hid, bw = refs[4:]
    dp, sub = place[1], place[2]
    patches = g0.shape[0]
    bytes_ = g0.shape[1] // DSLICE
    rows = patches * bytes_
    depth = bridge[0].shape[0]
    for b, ref in zip(block_order(dp, sub), bridge):
        bw[pl.ds(pl.multiple_of(b * depth, depth), depth), :] = ref[...]
    glob = (g0[...] + g1[...].astype(F32)).astype(BF16)
    stacked = jnp.concatenate(
        [glob[:, p * DSLICE : (p + 1) * DSLICE] for p in range(bytes_)], axis=0
    )
    to = lax.broadcasted_iota(jnp.int32, (rows, rows), 0)
    source = lax.broadcasted_iota(jnp.int32, (rows, rows), 1)
    pick = ((to % bytes_) * patches + to // bytes_ == source).astype(BF16)
    by_patch = dot(pick, stacked).astype(BF16)
    byte_in = embed[...].astype(F32) + dot(by_patch, bw[...])
    mean_square = jnp.mean(byte_in * byte_in, axis=1, keepdims=True)
    hid[...] = (byte_in * lax.rsqrt(mean_square + 1e-05) * gain[...]).astype(BF16)


def block_order(dp, sub):
    return [dp * 2 + sub, dp * 2 + 1 - sub, (1 - dp) * 2 + sub, (1 - dp) * 2 + 1 - sub]


def bytes_in(place, g0, g1, embed, gain, bridge):
    rows = embed.shape[0]
    return pl.pallas_call(
        bytes_kernel,
        out_shape=jax.ShapeDtypeStruct((rows, DL), BF16),
        in_specs=[SMEM] + [VMEM] * 8,
        out_specs=VMEM,
        scratch_shapes=[pltpu.VMEM((DSLICE, DL), BF16)],
        compiler_params=pltpu.CompilerParams(vmem_limit_bytes=10 * 2**20),
        cost_estimate=pl.CostEstimate(
            flops=2 * rows * DL * DSLICE, bytes_accessed=6 * rows * DL, transcendentals=rows
        ),
    )(place, g0, g1, embed, gain, *bridge)


def local_kernel(place, hid, *refs, pieces):
    whole = refs[:2]
    parts = refs[2 : 2 + 4 * pieces]
    out, held, sems = refs[2 + 4 * pieces :]
    dp, sub, grp = place[1], place[2], place[3]
    width = whole[0].shape[1]
    copies = []
    for i, b in enumerate(block_order(dp, sub)):
        if i < 2:
            total = dot(hid[...], whole[i][...])
        else:
            total = None
            for j in range(2):
                first = (grp if j == 0 else 1 - grp) * (hid.shape[1] // 2)
                for n in range(pieces):
                    ref = parts[((i - 2) * 2 + j) * pieces + n]
                    depth = ref.shape[0]
                    lhs = hid[:, pl.ds(pl.multiple_of(first, 128), depth)]
                    first += depth
                    term = dot(lhs, ref[...])
                    total = term if total is None else total + term
        held[i, :, :] = total.astype(BF16)
        copy = pltpu.make_async_copy(
            held.at[i], out.at[:, pl.ds(pl.multiple_of(b * width, 128), width)], sems.at[i]
        )
        copy.start()
        copies.append(copy)
    for copy in copies:
        copy.wait()


def local(place, hid, whole, parts):
    rows = hid.shape[0]
    block = whole[0].shape[1]
    pieces = len(parts) // 4
    return pl.pallas_call(
        functools.partial(local_kernel, pieces=pieces),
        out_shape=jax.ShapeDtypeStruct((rows, 4 * block), BF16),
        in_specs=[SMEM] + [VMEM] * (3 + len(parts)),
        out_specs=pl.BlockSpec(memory_space=pl.ANY),
        scratch_shapes=[pltpu.VMEM((4, rows, block), BF16), pltpu.SemaphoreType.DMA((4,))],
        compiler_params=pltpu.CompilerParams(vmem_limit_bytes=12 * 2**20),
        cost_estimate=pl.CostEstimate(
            flops=8 * rows * DL * block,
            bytes_accessed=8 * DL * block + 8 * rows * block,
            transcendentals=0,
        ),
    )(place, hid, *whole, *parts)


def swap(x, axis):
    return lax.ppermute(x, axis, [(0, 1), (1, 0)])


def after(x, *events):
    return lax.optimization_barrier((x, *events))[0]


def small_mesh(
    q_glob, k_glob, v_glob, x_glob, out_weight, bridge_weight, byte_embed, norm_gain, qkv_weight
):
    ctx, dp, sub, grp = (lax.axis_index(a) for a in ("ctx", "dp", "sub", "groups"))
    place = jnp.stack([ctx, dp, sub, grp]).astype(jnp.int32)

    quarter = qkv_weight.shape[0] // 4
    held = hold(q_glob, k_glob, v_glob)
    w0 = lax.dynamic_slice_in_dim(qkv_weight, grp * 2 * quarter, quarter, 0)
    w1 = lax.dynamic_slice_in_dim(after(qkv_weight, held), (grp * 2 + 1) * quarter, quarter, 0)

    x0 = swap(w0, "dp")
    q_up = lax.ppermute(q_glob, "ctx", [(2, 0), (3, 1)])
    k_low = lax.ppermute(k_glob, "ctx", [(0, 1), (1, 2), (2, 3)])
    v_low = lax.ppermute(v_glob, "ctx", [(0, 1), (1, 2), (2, 3)])
    q_up, k_low, v_low, x0, held, w1, bridge_weight, qkv_weight, place = (
        lax.optimization_barrier(
            (q_up, k_low, v_low, x0, held, w1, bridge_weight, qkv_weight, place)
        )
    )

    own, own_log, up = attend(place, held, q_up, k_low, v_low)
    low = lax.ppermute(up, "ctx", [(0, 2), (1, 3)])
    x1 = swap(w1, "dp")
    y0 = swap(x0, "groups")
    other_core = swap(qkv_weight, "sub")
    out_weight = bring(after(out_weight, up), 4)
    bridge_x = swap(bridge_weight, "dp")
    low, x0, x1, y0, other_core, out_weight = lax.optimization_barrier(
        (low, x0, x1, y0, other_core, out_weight)
    )

    away, kept = project(place, own, own_log, low, x_glob, out_weight)
    away = swap(away, "sub")
    y1 = swap(x1, "groups")
    bridge_both = swap(bridge_x, "sub")
    core_y0 = swap(y0, "sub")
    away, core_y0, bridge_both, x0, x1, bridge_weight = lax.optimization_barrier(
        (away, core_y0, bridge_both, x0, x1, bridge_weight)
    )

    summed = kept + away.astype(F32)
    mid = summed.shape[0] // 2
    across = swap(summed[:mid].astype(BF16), "dp")
    core_x1 = swap(x1, "sub")
    bridge_core = swap(bridge_weight, "sub")
    core_x0 = swap(x0, "sub")
    across, y1, core_x0, core_x1, bridge_core = lax.optimization_barrier(
        (across, y1, core_x0, core_x1, bridge_core)
    )

    core_y1 = swap(y1, "sub")
    rows = byte_embed.shape[0] * byte_embed.shape[1]
    hidden = bytes_in(
        place,
        summed[mid:],
        across,
        byte_embed.reshape(rows, DL),
        norm_gain.reshape(1, DL),
        [bridge_weight, bridge_core, bridge_x, bridge_both],
    )
    result = local(
        place,
        hidden,
        [qkv_weight, other_core],
        [x0, x1, y0, y1, core_x0, core_x1, core_y0, core_y1],
    )
    return result.reshape(byte_embed.shape[0], P_SIZE, result.shape[1])


def solution(mesh):
    rows = P(("groups", "ctx"), GROUP)
    in_specs = (
        rows,
        rows,
        rows,
        rows,
        P(GROUP, None),
        P(GROUP, None),
        P(("groups", "ctx", "dp", "sub"), None, None),
        P(),
        P(None, GROUP),
    )
    out_specs = P(("groups", "ctx", "dp", "sub"), None, None)
    pairs = all(mesh.shape[a] == 2 for a in ("groups", "dp", "sub"))
    per_device = small_mesh if pairs and mesh.shape["ctx"] == 4 else any_mesh
    return jax.shard_map(
        per_device, mesh=mesh, in_specs=in_specs, out_specs=out_specs, check_vma=False
    )
```

```python
import functools
import math

import jax
import jax.numpy as jnp
from jax import lax
from jax.experimental import pallas as pl
from jax.experimental.pallas import tpu as pltpu
from jax.sharding import PartitionSpec as P

HD = 128
DL = 1024
P_SIZE = 8
DSLICE = 512
GROUP = ("dp", "sub")
SCALE = 1.0 / math.sqrt(HD)
VMEM = pl.BlockSpec(memory_space=pltpu.VMEM)
HBM = pl.BlockSpec(memory_space=pltpu.HBM)
F32 = jnp.float32
BF16 = jnp.bfloat16


def dot(a, b):
    return jnp.dot(a, b, preferred_element_type=F32)


def any_mesh(
    q_glob, k_glob, v_glob, x_glob, out_weight, bridge_weight, byte_embed, norm_gain, qkv_weight
):
    query_rows, query_width = q_glob.shape
    head_count = query_width // HD
    first_row = lax.axis_index("ctx") * query_rows
    queries = q_glob.reshape(query_rows, head_count, HD)
    query_pos = first_row + lax.iota(jnp.int32, query_rows)
    keys = lax.all_gather(k_glob, "ctx", axis=0, tiled=True)
    values = lax.all_gather(v_glob, "ctx", axis=0, tiled=True)
    count = keys.shape[0]
    keys = keys.reshape(count, head_count, HD)
    values = values.reshape(count, head_count, HD)
    scores = jnp.einsum("qhd,khd->hqk", queries, keys, preferred_element_type=F32) * SCALE
    allowed = query_pos[:, None] >= lax.iota(jnp.int32, count)[None, :]
    scores = jnp.where(allowed[None], scores, -jnp.inf)
    weights = jnp.exp(scores - jnp.max(scores, axis=2)[:, :, None])
    row_sum = jnp.sum(weights, axis=2)
    weighted = jnp.einsum("hqk,khd->hqd", weights.astype(BF16), values, preferred_element_type=F32)
    attn = (weighted / row_sum[:, :, None]).astype(BF16)
    attn = attn.transpose(1, 0, 2).reshape(query_rows, query_width)
    head_terms = dot(attn, out_weight)
    own_bytes = P_SIZE // lax.axis_size(GROUP)
    feature_sum = lax.psum_scatter(
        head_terms.astype(BF16), GROUP, scatter_dimension=1, tiled=True
    ).astype(F32)
    patch_out = (feature_sum + x_glob.astype(F32)).astype(BF16)
    patch_out = patch_out.reshape(query_rows, own_bytes, DSLICE)
    patch_out = lax.all_to_all(patch_out, GROUP, split_axis=0, concat_axis=1, tiled=True)
    glob_bytes = patch_out.reshape(-1, DSLICE)
    byte_rows = glob_bytes.shape[0]
    bridged = dot(glob_bytes, lax.all_gather(bridge_weight, GROUP, axis=0, tiled=True))
    byte_in = byte_embed.reshape(byte_rows, DL).astype(F32) + bridged
    mean_square = jnp.mean(byte_in * byte_in, axis=1, keepdims=True)
    normalized = (byte_in * lax.rsqrt(mean_square + 1e-05) * norm_gain).astype(BF16)
    result = dot(normalized, lax.all_gather(qkv_weight, GROUP, axis=1, tiled=True)).astype(BF16)
    return result.reshape(byte_embed.shape[0], P_SIZE, 3 * DL)


def attend_kernel(held, q_up, k_low, v_low, own, own_log, up):
    rows, width = q_up.shape
    heads = width // HD
    has_low = lax.axis_index("ctx") >= 1
    row = lax.broadcasted_iota(jnp.int32, (rows, 2 * rows), 0)
    col = lax.broadcasted_iota(jnp.int32, (rows, 2 * rows), 1)
    low = jnp.logical_and(col >= rows, has_low)
    full = jnp.logical_or(col < rows, low)
    causal = jnp.logical_or(row >= col, low)
    logs = [[], []]
    for h in range(heads):
        cols = pl.ds(h * HD, HD)
        qh, k, v = (held[:, pl.ds(i * width + h * HD, HD)] for i in range(3))
        kh = jnp.concatenate([k, k_low[:, cols]], axis=0)
        vh = jnp.concatenate([v, v_low[:, cols]], axis=0)
        for i, (queries, mask, target) in enumerate(((qh, causal, own), (q_up[:, cols], full, up))):
            scores = lax.dot_general(
                queries, kh, (((1,), (1,)), ((), ())), preferred_element_type=F32
            ) * SCALE
            scores = jnp.where(mask, scores, -jnp.inf)
            top = jnp.max(scores, axis=1, keepdims=True)
            probs = jnp.exp(scores - top)
            total = jnp.sum(probs, axis=1, keepdims=True)
            mixed = dot(probs.astype(BF16), vh) / total
            target[pl.ds(0, rows), cols] = mixed.astype(target.dtype)
            logs[i].append(top + jnp.log(total))
    lane = lax.broadcasted_iota(jnp.int32, (rows, HD), 1)

    def by_lane(columns):
        table = jnp.zeros((rows, HD), F32)
        for i, column in enumerate(columns):
            table = jnp.where(lane == i, column, table)
        return table

    own_log[...] = by_lane(logs[0])
    terms = []
    rest = logs[1]
    for _ in range(3):
        high = [r.astype(BF16).astype(F32) for r in rest]
        rest = [r - t for r, t in zip(rest, high)]
        terms += high
    up[pl.ds(rows, 16), :] = jnp.zeros((16, width), BF16)
    up[pl.ds(rows, 16), pl.ds(0, HD)] = by_lane(terms).T[:16, :rows].astype(BF16)


def attend(held, q_up, k_low, v_low):
    rows, width = q_up.shape
    return pl.pallas_call(
        attend_kernel,
        out_shape=(
            jax.ShapeDtypeStruct((rows, width), F32),
            jax.ShapeDtypeStruct((rows, HD), F32),
            jax.ShapeDtypeStruct((rows + 16, width), BF16),
        ),
        in_specs=[VMEM] * 4,
        out_specs=(VMEM,) * 3,
        compiler_params=pltpu.CompilerParams(vmem_limit_bytes=6 * 2**20),
        cost_estimate=pl.CostEstimate(
            flops=16 * rows * rows * width,
            bytes_accessed=24 * rows * width,
            transcendentals=4 * rows * rows * width // HD,
        ),
    )(held, q_up, k_low, v_low)


def copy_all(pairs, sems):
    copies = [pltpu.make_async_copy(a, b, sems.at[i]) for i, (a, b) in enumerate(pairs)]
    for copy in copies:
        copy.start()
    for copy in copies:
        copy.wait()


def hold_kernel(q, k, v, held):
    width = q.shape[1]
    for i, source in enumerate((q, k, v)):
        held[:, pl.ds(i * width, width)] = source[...]


def hold(q, k, v):
    return pl.pallas_call(
        hold_kernel,
        out_shape=jax.ShapeDtypeStruct((q.shape[0], 3 * q.shape[1]), q.dtype),
        in_specs=[VMEM] * 3,
        out_specs=VMEM,
        compiler_params=pltpu.CompilerParams(vmem_limit_bytes=2 * 2**20),
    )(q, k, v)


def bring_kernel(source, target, sems):
    rows = source.shape[0] // sems.shape[0]
    cuts = [pl.ds(i * rows, rows) for i in range(sems.shape[0])]
    copy_all([(source.at[c, :], target.at[c, :]) for c in cuts], sems)


def bring(x, parts):
    return pl.pallas_call(
        bring_kernel,
        out_shape=jax.ShapeDtypeStruct(x.shape, x.dtype),
        in_specs=[HBM],
        out_specs=VMEM,
        scratch_shapes=[pltpu.SemaphoreType.DMA((parts,))],
        compiler_params=pltpu.CompilerParams(vmem_limit_bytes=2 * 2**20),
    )(x)


def project_kernel(own, own_log, low, x, w, away, kept, attn, xs):
    ctx, dp, sub = lax.axis_index("ctx"), lax.axis_index("dp"), lax.axis_index("sub")
    rows, width = own.shape
    heads = width // HD
    quarter = rows // 4
    table = low[pl.ds(rows, 16), pl.ds(0, HD)].astype(F32)
    table = jnp.concatenate([table, jnp.zeros((HD - 16, HD), F32)], axis=0).T
    for h in range(heads):
        cols = pl.ds(h * HD, HD)
        log = own_log[:, h : h + 1]
        log_low = (
            table[:, h : h + 1]
            + table[:, heads + h : heads + h + 1]
            + table[:, 2 * heads + h : 2 * heads + h + 1]
        )
        log_low = jnp.where(ctx >= 2, log_low, -jnp.inf)
        top = jnp.maximum(log, log_low)
        share, share_low = jnp.exp(log - top), jnp.exp(log_low - top)
        mixed = share * own[:, cols] + share_low * low[pl.ds(0, rows), cols].astype(F32)
        attn[:, cols] = (mixed / (share + share_low)).astype(BF16)
    order = []
    for core in (1 - sub, sub):
        for chip in (1 - dp, dp):
            order.append(pl.ds(pl.multiple_of((chip * 2 + core) * quarter, quarter), quarter))
    a = jnp.concatenate([attn[o, :] for o in order], axis=0)
    for i, o in enumerate(order):
        xs[pl.ds(i * quarter, quarter), :] = x[o, :]
    block = x.shape[1]
    mine = dp * 2 + sub
    for b in range(w.shape[1] // block):
        cols = pl.ds(b * block, block)
        terms = dot(a, w[:, cols])
        terms += jnp.where(mine == b, xs[...].astype(F32), 0.0)
        away[:, cols] = terms[: 2 * quarter].astype(BF16)
        kept[:, cols] = terms[2 * quarter :]


def project(own, own_log, low, x, w):
    rows, width = own.shape
    half = rows // 2
    return pl.pallas_call(
        project_kernel,
        out_shape=(
            jax.ShapeDtypeStruct((half, w.shape[1]), BF16),
            jax.ShapeDtypeStruct((half, w.shape[1]), F32),
        ),
        in_specs=[VMEM] * 5,
        out_specs=(VMEM, VMEM),
        scratch_shapes=[pltpu.VMEM((rows, width), BF16), pltpu.VMEM(x.shape, BF16)],
        compiler_params=pltpu.CompilerParams(vmem_limit_bytes=12 * 2**20),
        cost_estimate=pl.CostEstimate(
            flops=2 * rows * width * w.shape[1],
            bytes_accessed=2 * w.size + 6 * half * w.shape[1],
            transcendentals=3 * rows * width // HD,
        ),
    )(own, own_log, low, x, w)


def sum_kernel(kept, away, send, stay):
    rows = send.shape[0]
    summed = kept[...] + away[...].astype(F32)
    send[...] = summed[:rows].astype(BF16)
    stay[...] = summed[rows:]


def sum_cores(kept, away):
    rows, width = kept.shape[0] // 2, kept.shape[1]
    return pl.pallas_call(
        sum_kernel,
        out_shape=(
            jax.ShapeDtypeStruct((rows, width), BF16),
            jax.ShapeDtypeStruct((rows, width), F32),
        ),
        in_specs=[VMEM] * 2,
        out_specs=(VMEM,) * 2,
        compiler_params=pltpu.CompilerParams(vmem_limit_bytes=2 * 2**20),
    )(kept, away)


def bytes_kernel(g0, g1, embed, gain, *refs):
    bridge = refs[:4]
    hid, turned, bw = refs[4:]
    dp, sub, grp = lax.axis_index("dp"), lax.axis_index("sub"), lax.axis_index("groups")
    patches = g0.shape[0]
    bytes_ = g0.shape[1] // DSLICE
    rows = patches * bytes_
    depth = bridge[0].shape[0]
    for b, ref in zip(block_order(dp, sub), bridge):
        bw[pl.ds(pl.multiple_of(b * depth, depth), depth), :] = ref[...]
    glob = (g0[...] + g1[...].astype(F32)).astype(BF16)
    stacked = jnp.concatenate(
        [glob[:, p * DSLICE : (p + 1) * DSLICE] for p in range(bytes_)], axis=0
    )
    to = lax.broadcasted_iota(jnp.int32, (rows, rows), 0)
    source = lax.broadcasted_iota(jnp.int32, (rows, rows), 1)
    pick = ((to % bytes_) * patches + to // bytes_ == source).astype(BF16)
    by_patch = dot(pick, stacked).astype(BF16)
    byte_in = embed[...].astype(F32) + dot(by_patch, bw[...])
    mean_square = jnp.mean(byte_in * byte_in, axis=1, keepdims=True)
    normalized = (byte_in * lax.rsqrt(mean_square + 1e-05) * gain[...]).astype(BF16)
    hid[...] = normalized
    half = normalized.shape[1] // 2
    turned[:, pl.ds(pl.multiple_of(grp * half, half), half)] = normalized[:, :half]
    turned[:, pl.ds(pl.multiple_of((1 - grp) * half, half), half)] = normalized[:, half:]


def block_order(dp, sub):
    return [dp * 2 + sub, dp * 2 + 1 - sub, (1 - dp) * 2 + sub, (1 - dp) * 2 + 1 - sub]


def bytes_in(g0, g1, embed, gain, bridge):
    rows = embed.shape[0]
    return pl.pallas_call(
        bytes_kernel,
        out_shape=(jax.ShapeDtypeStruct((rows, DL), BF16),) * 2,
        in_specs=[VMEM] * 8,
        out_specs=(VMEM,) * 2,
        scratch_shapes=[pltpu.VMEM((DSLICE, DL), BF16)],
        compiler_params=pltpu.CompilerParams(vmem_limit_bytes=10 * 2**20),
        cost_estimate=pl.CostEstimate(
            flops=2 * rows * DL * DSLICE, bytes_accessed=6 * rows * DL, transcendentals=rows
        ),
    )(g0, g1, embed, gain, *bridge)


def local_kernel(hid, turned, *refs, counts):
    dp, sub = lax.axis_index("dp"), lax.axis_index("sub")
    width = refs[0].shape[1]
    out, held, sems = refs[sum(counts) :]
    copies, at = [], 0
    for i, b in enumerate(block_order(dp, sub)):
        source = hid if counts[i] == 1 else turned
        total, row = None, 0
        for ref in refs[at : at + counts[i]]:
            term = dot(source[:, row : row + ref.shape[0]], ref[...])
            total = term if total is None else total + term
            row += ref.shape[0]
        at += counts[i]
        held[i, :, :] = total.astype(BF16)
        copy = pltpu.make_async_copy(
            held.at[i], out.at[:, pl.ds(pl.multiple_of(b * width, 128), width)], sems.at[i]
        )
        copy.start()
        copies.append(copy)
    for copy in copies:
        copy.wait()


def local(hid, turned, *blocks):
    rows = hid.shape[0]
    weights = [piece for block in blocks for piece in block]
    width = weights[0].shape[1]
    return pl.pallas_call(
        functools.partial(local_kernel, counts=tuple(len(block) for block in blocks)),
        out_shape=jax.ShapeDtypeStruct((rows, 4 * width), BF16),
        in_specs=[VMEM] * (2 + len(weights)),
        out_specs=pl.BlockSpec(memory_space=pl.ANY),
        scratch_shapes=[pltpu.VMEM((4, rows, width), BF16), pltpu.SemaphoreType.DMA((4,))],
        compiler_params=pltpu.CompilerParams(vmem_limit_bytes=12 * 2**20),
    )(hid, turned, *weights)


def swap(x, axis):
    return lax.ppermute(x, axis, [(0, 1), (1, 0)])


def after(x, *events):
    return lax.optimization_barrier((x, *events))[0]


def small_mesh(
    q_glob, k_glob, v_glob, x_glob, out_weight, bridge_weight, byte_embed, norm_gain, qkv_weight
):
    grp = lax.axis_index("groups")

    quarter = qkv_weight.shape[0] // 4
    held = hold(q_glob, k_glob, v_glob)
    w0 = lax.dynamic_slice_in_dim(qkv_weight, grp * 2 * quarter, quarter, 0)
    w1 = lax.dynamic_slice_in_dim(after(qkv_weight, held), (grp * 2 + 1) * quarter, quarter, 0)

    x0 = swap(w0, "dp")
    bridge_x = swap(bridge_weight, "dp")
    q_up = lax.ppermute(q_glob, "ctx", [(2, 0), (3, 1)])
    k_low = lax.ppermute(k_glob, "ctx", [(0, 1), (1, 2), (2, 3)])
    v_low = lax.ppermute(v_glob, "ctx", [(0, 1), (1, 2), (2, 3)])
    q_up, k_low, v_low, x0, bridge_x, held, w1, bridge_weight, qkv_weight = (
        lax.optimization_barrier(
            (q_up, k_low, v_low, x0, bridge_x, held, w1, bridge_weight, qkv_weight)
        )
    )

    own, own_log, up = attend(held, q_up, k_low, v_low)
    low = lax.ppermute(up, "ctx", [(0, 2), (1, 3)])
    x1 = swap(w1, "dp")
    y0 = swap(x0, "groups")
    other_core = swap(qkv_weight, "sub")
    core_x0 = swap(x0, "sub")
    out_weight = bring(after(out_weight, up), 4)
    low, core_x0, x1, other_core, out_weight, bridge_x = lax.optimization_barrier(
        (low, core_x0, x1, other_core, out_weight, bridge_x)
    )

    away, kept = project(own, own_log, low, x_glob, out_weight)
    away = swap(away, "sub")
    y1 = swap(x1, "groups")
    bridge_both = swap(bridge_x, "sub")
    core_y0 = swap(y0, "sub")
    away, core_y0, bridge_both, x1, bridge_weight = lax.optimization_barrier(
        (away, core_y0, bridge_both, x1, bridge_weight)
    )

    send, stay = sum_cores(kept, away)
    across = swap(send, "dp")
    core_x1 = swap(x1, "sub")
    bridge_core = swap(bridge_weight, "sub")
    across, y1, core_x1, bridge_core = lax.optimization_barrier(
        (across, y1, core_x1, bridge_core)
    )

    core_y1 = swap(y1, "sub")
    rows = byte_embed.shape[0] * byte_embed.shape[1]
    hidden, turned = bytes_in(
        stay,
        across,
        byte_embed.reshape(rows, DL),
        norm_gain.reshape(1, DL),
        [bridge_weight, bridge_core, bridge_x, bridge_both],
    )
    result = local(
        hidden,
        turned,
        [qkv_weight],
        [other_core],
        [x0, x1, y0, y1],
        [core_x0, core_x1, core_y0, core_y1],
    )
    return result.reshape(byte_embed.shape[0], P_SIZE, result.shape[1])


def solution(mesh):
    rows = P(("groups", "ctx"), GROUP)
    in_specs = (
        rows,
        rows,
        rows,
        rows,
        P(GROUP, None),
        P(GROUP, None),
        P(("groups", "ctx", "dp", "sub"), None, None),
        P(),
        P(None, GROUP),
    )
    out_specs = P(("groups", "ctx", "dp", "sub"), None, None)
    pairs = all(mesh.shape[a] == 2 for a in ("groups", "dp", "sub"))
    per_device = small_mesh if pairs and mesh.shape["ctx"] == 4 else any_mesh
    return jax.shard_map(
        per_device, mesh=mesh, in_specs=in_specs, out_specs=out_specs, check_vma=False
    )
```

```python
import functools
import math

import jax
import jax.numpy as jnp
from jax import lax
from jax.experimental import pallas as pl
from jax.experimental.pallas import tpu as pltpu
from jax.sharding import PartitionSpec as P

HD = 128
DL = 1024
P_SIZE = 8
DSLICE = 512
GROUP = ("dp", "sub")
SCALE = 1.0 / math.sqrt(HD)
VMEM = pl.BlockSpec(memory_space=pltpu.VMEM)
HBM = pl.BlockSpec(memory_space=pltpu.HBM)
F32 = jnp.float32
BF16 = jnp.bfloat16


def dot(a, b):
    return jnp.dot(a, b, preferred_element_type=F32)


def any_mesh(
    q_glob, k_glob, v_glob, x_glob, out_weight, bridge_weight, byte_embed, norm_gain, qkv_weight
):
    query_rows, query_width = q_glob.shape
    head_count = query_width // HD
    first_row = lax.axis_index("ctx") * query_rows
    queries = q_glob.reshape(query_rows, head_count, HD)
    query_pos = first_row + lax.iota(jnp.int32, query_rows)
    keys = lax.all_gather(k_glob, "ctx", axis=0, tiled=True)
    values = lax.all_gather(v_glob, "ctx", axis=0, tiled=True)
    count = keys.shape[0]
    keys = keys.reshape(count, head_count, HD)
    values = values.reshape(count, head_count, HD)
    scores = jnp.einsum("qhd,khd->hqk", queries, keys, preferred_element_type=F32) * SCALE
    allowed = query_pos[:, None] >= lax.iota(jnp.int32, count)[None, :]
    scores = jnp.where(allowed[None], scores, -jnp.inf)
    weights = jnp.exp(scores - jnp.max(scores, axis=2)[:, :, None])
    row_sum = jnp.sum(weights, axis=2)
    weighted = jnp.einsum("hqk,khd->hqd", weights.astype(BF16), values, preferred_element_type=F32)
    attn = (weighted / row_sum[:, :, None]).astype(BF16)
    attn = attn.transpose(1, 0, 2).reshape(query_rows, query_width)
    head_terms = dot(attn, out_weight)
    own_bytes = P_SIZE // lax.axis_size(GROUP)
    feature_sum = lax.psum_scatter(
        head_terms.astype(BF16), GROUP, scatter_dimension=1, tiled=True
    ).astype(F32)
    patch_out = (feature_sum + x_glob.astype(F32)).astype(BF16)
    patch_out = patch_out.reshape(query_rows, own_bytes, DSLICE)
    patch_out = lax.all_to_all(patch_out, GROUP, split_axis=0, concat_axis=1, tiled=True)
    glob_bytes = patch_out.reshape(-1, DSLICE)
    byte_rows = glob_bytes.shape[0]
    bridged = dot(glob_bytes, lax.all_gather(bridge_weight, GROUP, axis=0, tiled=True))
    byte_in = byte_embed.reshape(byte_rows, DL).astype(F32) + bridged
    mean_square = jnp.mean(byte_in * byte_in, axis=1, keepdims=True)
    normalized = (byte_in * lax.rsqrt(mean_square + 1e-05) * norm_gain).astype(BF16)
    result = dot(normalized, lax.all_gather(qkv_weight, GROUP, axis=1, tiled=True)).astype(BF16)
    return result.reshape(byte_embed.shape[0], P_SIZE, 3 * DL)


def attend_block(queries, held, k_low, v_low, h, mask, target):
    rows = queries.shape[0]
    width = k_low.shape[1]
    cols = pl.ds(h * HD, HD)
    k, v = (held[:, pl.ds(i * width + h * HD, HD)] for i in (1, 2))
    kh = jnp.concatenate([k, k_low[:, cols]], axis=0)
    vh = jnp.concatenate([v, v_low[:, cols]], axis=0)
    scores = lax.dot_general(
        queries[:, cols], kh, (((1,), (1,)), ((), ())), preferred_element_type=F32
    ) * SCALE
    scores = jnp.where(mask, scores, -jnp.inf)
    top = jnp.max(scores, axis=1, keepdims=True)
    probs = jnp.exp(scores - top)
    total = jnp.sum(probs, axis=1, keepdims=True)
    mixed = dot(probs.astype(BF16), vh) / total
    target[pl.ds(0, rows), cols] = mixed.astype(target.dtype)
    return top + jnp.log(total)


def masks(rows):
    row = lax.broadcasted_iota(jnp.int32, (rows, 2 * rows), 0)
    col = lax.broadcasted_iota(jnp.int32, (rows, 2 * rows), 1)
    low = jnp.logical_and(col >= rows, lax.axis_index("ctx") >= 1)
    return col < rows, low, row >= col


def by_lane(columns):
    rows = columns[0].shape[0]
    lane = lax.broadcasted_iota(jnp.int32, (rows, HD), 1)
    table = jnp.zeros((rows, HD), F32)
    for i, column in enumerate(columns):
        table = jnp.where(lane == i, column, table)
    return table


def attend_own_kernel(held, k_low, v_low, own, own_log):
    _, low, causal = masks(own.shape[0])
    mask = jnp.logical_or(causal, low)
    heads = range(own.shape[1] // HD)
    own_log[...] = by_lane([attend_block(held, held, k_low, v_low, h, mask, own) for h in heads])


def attend_up_kernel(held, q_up, k_low, v_low, up):
    rows, width = q_up.shape
    here, low, _ = masks(rows)
    mask = jnp.logical_or(here, low)
    rest = [attend_block(q_up, held, k_low, v_low, h, mask, up) for h in range(width // HD)]
    terms = []
    for _ in range(3):
        high = [r.astype(BF16).astype(F32) for r in rest]
        rest = [r - t for r, t in zip(rest, high)]
        terms += high
    up[pl.ds(rows, 16), :] = jnp.zeros((16, width), BF16)
    up[pl.ds(rows, 16), pl.ds(0, HD)] = by_lane(terms).T[:16, :rows].astype(BF16)


def attend_own(held, k_low, v_low):
    rows, width = k_low.shape
    return pl.pallas_call(
        attend_own_kernel,
        out_shape=(
            jax.ShapeDtypeStruct((rows, width), F32),
            jax.ShapeDtypeStruct((rows, HD), F32),
        ),
        in_specs=[VMEM] * 3,
        out_specs=(VMEM,) * 2,
        compiler_params=pltpu.CompilerParams(vmem_limit_bytes=6 * 2**20),
    )(held, k_low, v_low)


def attend_up(held, q_up, k_low, v_low):
    rows, width = q_up.shape
    return pl.pallas_call(
        attend_up_kernel,
        out_shape=jax.ShapeDtypeStruct((rows + 16, width), BF16),
        in_specs=[VMEM] * 4,
        out_specs=VMEM,
        compiler_params=pltpu.CompilerParams(vmem_limit_bytes=6 * 2**20),
    )(held, q_up, k_low, v_low)


def copy_all(pairs, sems):
    copies = [pltpu.make_async_copy(a, b, sems.at[i]) for i, (a, b) in enumerate(pairs)]
    for copy in copies:
        copy.start()
    for copy in copies:
        copy.wait()


def hold_kernel(q, k, v, held):
    width = q.shape[1]
    for i, source in enumerate((q, k, v)):
        held[:, pl.ds(i * width, width)] = source[...]


def hold(q, k, v):
    return pl.pallas_call(
        hold_kernel,
        out_shape=jax.ShapeDtypeStruct((q.shape[0], 3 * q.shape[1]), q.dtype),
        in_specs=[VMEM] * 3,
        out_specs=VMEM,
        compiler_params=pltpu.CompilerParams(vmem_limit_bytes=2 * 2**20),
    )(q, k, v)


def bring_kernel(source, target, sems):
    rows = source.shape[0] // sems.shape[0]
    cuts = [pl.ds(i * rows, rows) for i in range(sems.shape[0])]
    copy_all([(source.at[c, :], target.at[c, :]) for c in cuts], sems)


def bring(x, parts):
    return pl.pallas_call(
        bring_kernel,
        out_shape=jax.ShapeDtypeStruct(x.shape, x.dtype),
        in_specs=[HBM],
        out_specs=VMEM,
        scratch_shapes=[pltpu.SemaphoreType.DMA((parts,))],
        compiler_params=pltpu.CompilerParams(vmem_limit_bytes=2 * 2**20),
    )(x)


def project_kernel(own, own_log, low, x, w, away, kept, attn, xs):
    ctx, dp, sub = lax.axis_index("ctx"), lax.axis_index("dp"), lax.axis_index("sub")
    rows, width = own.shape
    heads = width // HD
    quarter = rows // 4
    table = low[pl.ds(rows, 16), pl.ds(0, HD)].astype(F32)
    table = jnp.concatenate([table, jnp.zeros((HD - 16, HD), F32)], axis=0).T
    for h in range(heads):
        cols = pl.ds(h * HD, HD)
        log = own_log[:, h : h + 1]
        log_low = (
            table[:, h : h + 1]
            + table[:, heads + h : heads + h + 1]
            + table[:, 2 * heads + h : 2 * heads + h + 1]
        )
        log_low = jnp.where(ctx >= 2, log_low, -jnp.inf)
        top = jnp.maximum(log, log_low)
        share, share_low = jnp.exp(log - top), jnp.exp(log_low - top)
        mixed = share * own[:, cols] + share_low * low[pl.ds(0, rows), cols].astype(F32)
        attn[:, cols] = (mixed / (share + share_low)).astype(BF16)
    order = []
    for core in (1 - sub, sub):
        for chip in (1 - dp, dp):
            order.append(pl.ds(pl.multiple_of((chip * 2 + core) * quarter, quarter), quarter))
    a = jnp.concatenate([attn[o, :] for o in order], axis=0)
    for i, o in enumerate(order):
        xs[pl.ds(i * quarter, quarter), :] = x[o, :]
    block = x.shape[1]
    mine = dp * 2 + sub
    for b in range(w.shape[1] // block):
        cols = pl.ds(b * block, block)
        terms = dot(a, w[:, cols])
        terms += jnp.where(mine == b, xs[...].astype(F32), 0.0)
        away[:, cols] = terms[: 2 * quarter].astype(BF16)
        kept[:, cols] = terms[2 * quarter :]


def project(own, own_log, low, x, w):
    rows, width = own.shape
    half = rows // 2
    return pl.pallas_call(
        project_kernel,
        out_shape=(
            jax.ShapeDtypeStruct((half, w.shape[1]), BF16),
            jax.ShapeDtypeStruct((half, w.shape[1]), F32),
        ),
        in_specs=[VMEM] * 5,
        out_specs=(VMEM, VMEM),
        scratch_shapes=[pltpu.VMEM((rows, width), BF16), pltpu.VMEM(x.shape, BF16)],
        compiler_params=pltpu.CompilerParams(vmem_limit_bytes=12 * 2**20),
        cost_estimate=pl.CostEstimate(
            flops=2 * rows * width * w.shape[1],
            bytes_accessed=2 * w.size + 6 * half * w.shape[1],
            transcendentals=3 * rows * width // HD,
        ),
    )(own, own_log, low, x, w)


def sum_kernel(kept, away, send, stay):
    rows = send.shape[0]
    summed = kept[...] + away[...].astype(F32)
    send[...] = summed[:rows].astype(BF16)
    stay[...] = summed[rows:]


def sum_cores(kept, away):
    rows, width = kept.shape[0] // 2, kept.shape[1]
    return pl.pallas_call(
        sum_kernel,
        out_shape=(
            jax.ShapeDtypeStruct((rows, width), BF16),
            jax.ShapeDtypeStruct((rows, width), F32),
        ),
        in_specs=[VMEM] * 2,
        out_specs=(VMEM,) * 2,
        compiler_params=pltpu.CompilerParams(vmem_limit_bytes=2 * 2**20),
    )(kept, away)


def bytes_kernel(g0, g1, embed, gain, *refs):
    bridge, halves = refs[:2], refs[2:6]
    hid, turned, bw = refs[6:]
    dp, sub, grp = lax.axis_index("dp"), lax.axis_index("sub"), lax.axis_index("groups")
    patches = g0.shape[0]
    bytes_ = g0.shape[1] // DSLICE
    rows = patches * bytes_
    depth = bridge[0].shape[0]
    order = block_order(dp, sub)
    cut = halves[0].shape[0]
    for b, ref in zip(order[:2], bridge):
        bw[pl.ds(pl.multiple_of(b * depth, depth), depth), :] = ref[...]
    for i, ref in enumerate(halves):
        row = order[2 + i // 2] * depth + i % 2 * cut
        bw[pl.ds(pl.multiple_of(row, 32), ref.shape[0]), :] = ref[...]
    glob = (g0[...] + g1[...].astype(F32)).astype(BF16)
    stacked = jnp.concatenate(
        [glob[:, p * DSLICE : (p + 1) * DSLICE] for p in range(bytes_)], axis=0
    )
    to = lax.broadcasted_iota(jnp.int32, (rows, rows), 0)
    source = lax.broadcasted_iota(jnp.int32, (rows, rows), 1)
    pick = ((to % bytes_) * patches + to // bytes_ == source).astype(BF16)
    by_patch = dot(pick, stacked).astype(BF16)
    byte_in = embed[...].astype(F32) + dot(by_patch, bw[...])
    mean_square = jnp.mean(byte_in * byte_in, axis=1, keepdims=True)
    normalized = (byte_in * lax.rsqrt(mean_square + 1e-05) * gain[...]).astype(BF16)
    hid[...] = normalized
    half = normalized.shape[1] // 2
    turned[:, pl.ds(pl.multiple_of(grp * half, half), half)] = normalized[:, :half]
    turned[:, pl.ds(pl.multiple_of((1 - grp) * half, half), half)] = normalized[:, half:]


def block_order(dp, sub):
    return [dp * 2 + sub, dp * 2 + 1 - sub, (1 - dp) * 2 + sub, (1 - dp) * 2 + 1 - sub]


def bytes_in(g0, g1, embed, gain, bridge):
    rows = embed.shape[0]
    return pl.pallas_call(
        bytes_kernel,
        out_shape=(jax.ShapeDtypeStruct((rows, DL), BF16),) * 2,
        in_specs=[VMEM] * 10,
        out_specs=(VMEM,) * 2,
        scratch_shapes=[pltpu.VMEM((DSLICE, DL), BF16)],
        compiler_params=pltpu.CompilerParams(vmem_limit_bytes=10 * 2**20),
        cost_estimate=pl.CostEstimate(
            flops=2 * rows * DL * DSLICE, bytes_accessed=6 * rows * DL, transcendentals=rows
        ),
    )(g0, g1, embed, gain, *bridge)


def local_kernel(hid, turned, *refs, counts):
    dp, sub = lax.axis_index("dp"), lax.axis_index("sub")
    width = refs[0].shape[1]
    out, held, sems = refs[sum(counts) :]
    copies, at = [], 0
    for i, b in enumerate(block_order(dp, sub)):
        source = hid if counts[i] == 1 else turned
        total, row = None, 0
        for ref in refs[at : at + counts[i]]:
            term = dot(source[:, row : row + ref.shape[0]], ref[...])
            total = term if total is None else total + term
            row += ref.shape[0]
        at += counts[i]
        held[i, :, :] = total.astype(BF16)
        copy = pltpu.make_async_copy(
            held.at[i], out.at[:, pl.ds(pl.multiple_of(b * width, 128), width)], sems.at[i]
        )
        copy.start()
        copies.append(copy)
    for copy in copies:
        copy.wait()


def local(hid, turned, *blocks):
    rows = hid.shape[0]
    weights = [piece for block in blocks for piece in block]
    width = weights[0].shape[1]
    return pl.pallas_call(
        functools.partial(local_kernel, counts=tuple(len(block) for block in blocks)),
        out_shape=jax.ShapeDtypeStruct((rows, 4 * width), BF16),
        in_specs=[VMEM] * (2 + len(weights)),
        out_specs=pl.BlockSpec(memory_space=pl.ANY),
        scratch_shapes=[pltpu.VMEM((4, rows, width), BF16), pltpu.SemaphoreType.DMA((4,))],
        compiler_params=pltpu.CompilerParams(vmem_limit_bytes=12 * 2**20),
    )(hid, turned, *weights)


def swap(x, axis):
    return lax.ppermute(x, axis, [(0, 1), (1, 0)])


def after(x, *events):
    return lax.optimization_barrier((x, *events))[0]


def small_mesh(
    q_glob, k_glob, v_glob, x_glob, out_weight, bridge_weight, byte_embed, norm_gain, qkv_weight
):
    grp = lax.axis_index("groups")

    quarter = qkv_weight.shape[0] // 4
    held = hold(q_glob, k_glob, v_glob)
    w0 = lax.dynamic_slice_in_dim(qkv_weight, grp * 2 * quarter, quarter, 0)
    w1 = lax.dynamic_slice_in_dim(after(qkv_weight, held), (grp * 2 + 1) * quarter, quarter, 0)

    x0 = swap(w0, "dp")
    bridge_rows = bridge_weight.shape[0] // 4 * 3
    bridge_a = swap(bridge_weight[:bridge_rows], "dp")
    q_up = lax.ppermute(q_glob, "ctx", [(2, 0), (3, 1)])
    k_low = lax.ppermute(k_glob, "ctx", [(0, 1), (1, 2), (2, 3)])
    v_low = lax.ppermute(v_glob, "ctx", [(0, 1), (1, 2), (2, 3)])
    q_up, k_low, v_low, x0, bridge_a, held, w1, bridge_weight, qkv_weight = (
        lax.optimization_barrier(
            (q_up, k_low, v_low, x0, bridge_a, held, w1, bridge_weight, qkv_weight)
        )
    )

    up = attend_up(held, q_up, k_low, v_low)
    own, own_log = attend_own(held, k_low, v_low)
    low = lax.ppermute(up, "ctx", [(0, 2), (1, 3)])
    x1 = swap(w1, "dp")
    y0 = swap(x0, "groups")
    other_core = swap(qkv_weight, "sub")
    out_weight = bring(after(out_weight, up), 4)
    bridge_b = swap(bridge_weight[bridge_rows:], "dp")
    low, x0, x1, other_core, out_weight, bridge_a, bridge_b = lax.optimization_barrier(
        (low, x0, x1, other_core, out_weight, bridge_a, bridge_b)
    )

    away, kept = project(own, own_log, low, x_glob, out_weight)
    away = swap(away, "sub")
    y1 = swap(x1, "groups")
    core_bridge_a = swap(bridge_a, "sub")
    core_bridge_b = swap(bridge_b, "sub")
    core_y0 = swap(y0, "sub")
    away, core_y0, core_bridge_a, core_bridge_b, x0, x1, bridge_weight = lax.optimization_barrier(
        (away, core_y0, core_bridge_a, core_bridge_b, x0, x1, bridge_weight)
    )

    send, stay = sum_cores(kept, away)
    across = swap(send, "dp")
    core_x1 = swap(x1, "sub")
    bridge_core = swap(bridge_weight, "sub")
    core_x0 = swap(x0, "sub")
    across, y1, core_x0, core_x1, bridge_core = lax.optimization_barrier(
        (across, y1, core_x0, core_x1, bridge_core)
    )

    core_y1 = swap(y1, "sub")
    rows = byte_embed.shape[0] * byte_embed.shape[1]
    hidden, turned = bytes_in(
        stay,
        across,
        byte_embed.reshape(rows, DL),
        norm_gain.reshape(1, DL),
        [bridge_weight, bridge_core, bridge_a, bridge_b, core_bridge_a, core_bridge_b],
    )
    result = local(
        hidden,
        turned,
        [qkv_weight],
        [other_core],
        [x0, x1, y0, y1],
        [core_x0, core_x1, core_y0, core_y1],
    )
    return result.reshape(byte_embed.shape[0], P_SIZE, result.shape[1])


def solution(mesh):
    rows = P(("groups", "ctx"), GROUP)
    in_specs = (
        rows,
        rows,
        rows,
        rows,
        P(GROUP, None),
        P(GROUP, None),
        P(("groups", "ctx", "dp", "sub"), None, None),
        P(),
        P(None, GROUP),
    )
    out_specs = P(("groups", "ctx", "dp", "sub"), None, None)
    pairs = all(mesh.shape[a] == 2 for a in ("groups", "dp", "sub"))
    per_device = small_mesh if pairs and mesh.shape["ctx"] == 4 else any_mesh
    return jax.shard_map(
        per_device, mesh=mesh, in_specs=in_specs, out_specs=out_specs, check_vma=False
    )
```

```python
import functools
import math

import jax
import jax.numpy as jnp
from jax import lax
from jax.experimental import pallas as pl
from jax.experimental.pallas import tpu as pltpu
from jax.sharding import PartitionSpec as P

HD = 128
DL = 1024
P_SIZE = 8
DSLICE = 512
GROUP = ("dp", "sub")
SCALE = 1.0 / math.sqrt(HD)
VMEM = pl.BlockSpec(memory_space=pltpu.VMEM)
HBM = pl.BlockSpec(memory_space=pltpu.HBM)
F32 = jnp.float32
BF16 = jnp.bfloat16


def dot(a, b):
    return jnp.dot(a, b, preferred_element_type=F32)


def any_mesh(
    q_glob, k_glob, v_glob, x_glob, out_weight, bridge_weight, byte_embed, norm_gain, qkv_weight
):
    query_rows, query_width = q_glob.shape
    head_count = query_width // HD
    first_row = lax.axis_index("ctx") * query_rows
    queries = q_glob.reshape(query_rows, head_count, HD)
    query_pos = first_row + lax.iota(jnp.int32, query_rows)
    keys = lax.all_gather(k_glob, "ctx", axis=0, tiled=True)
    values = lax.all_gather(v_glob, "ctx", axis=0, tiled=True)
    count = keys.shape[0]
    keys = keys.reshape(count, head_count, HD)
    values = values.reshape(count, head_count, HD)
    scores = jnp.einsum("qhd,khd->hqk", queries, keys, preferred_element_type=F32) * SCALE
    allowed = query_pos[:, None] >= lax.iota(jnp.int32, count)[None, :]
    scores = jnp.where(allowed[None], scores, -jnp.inf)
    weights = jnp.exp(scores - jnp.max(scores, axis=2)[:, :, None])
    row_sum = jnp.sum(weights, axis=2)
    weighted = jnp.einsum("hqk,khd->hqd", weights.astype(BF16), values, preferred_element_type=F32)
    attn = (weighted / row_sum[:, :, None]).astype(BF16)
    attn = attn.transpose(1, 0, 2).reshape(query_rows, query_width)
    head_terms = dot(attn, out_weight)
    own_bytes = P_SIZE // lax.axis_size(GROUP)
    feature_sum = lax.psum_scatter(
        head_terms.astype(BF16), GROUP, scatter_dimension=1, tiled=True
    ).astype(F32)
    patch_out = (feature_sum + x_glob.astype(F32)).astype(BF16)
    patch_out = patch_out.reshape(query_rows, own_bytes, DSLICE)
    patch_out = lax.all_to_all(patch_out, GROUP, split_axis=0, concat_axis=1, tiled=True)
    glob_bytes = patch_out.reshape(-1, DSLICE)
    byte_rows = glob_bytes.shape[0]
    bridged = dot(glob_bytes, lax.all_gather(bridge_weight, GROUP, axis=0, tiled=True))
    byte_in = byte_embed.reshape(byte_rows, DL).astype(F32) + bridged
    mean_square = jnp.mean(byte_in * byte_in, axis=1, keepdims=True)
    normalized = (byte_in * lax.rsqrt(mean_square + 1e-05) * norm_gain).astype(BF16)
    result = dot(normalized, lax.all_gather(qkv_weight, GROUP, axis=1, tiled=True)).astype(BF16)
    return result.reshape(byte_embed.shape[0], P_SIZE, 3 * DL)


def attend_block(queries, held, k_low, v_low, h, mask, target):
    rows = queries.shape[0]
    width = k_low.shape[1]
    cols = pl.ds(h * HD, HD)
    k, v = (held[:, pl.ds(i * width + h * HD, HD)] for i in (1, 2))
    kh = jnp.concatenate([k, k_low[:, cols]], axis=0)
    vh = jnp.concatenate([v, v_low[:, cols]], axis=0)
    scores = lax.dot_general(
        queries[:, cols], kh, (((1,), (1,)), ((), ())), preferred_element_type=F32
    ) * SCALE
    scores = jnp.where(mask, scores, -jnp.inf)
    top = jnp.max(scores, axis=1, keepdims=True)
    probs = jnp.exp(scores - top)
    total = jnp.sum(probs, axis=1, keepdims=True)
    mixed = dot(probs.astype(BF16), vh) / total
    target[pl.ds(0, rows), cols] = mixed.astype(target.dtype)
    return top + jnp.log(total)


def masks(rows):
    row = lax.broadcasted_iota(jnp.int32, (rows, 2 * rows), 0)
    col = lax.broadcasted_iota(jnp.int32, (rows, 2 * rows), 1)
    low = jnp.logical_and(col >= rows, lax.axis_index("ctx") >= 1)
    return col < rows, low, row >= col


def by_lane(columns):
    rows = columns[0].shape[0]
    lane = lax.broadcasted_iota(jnp.int32, (rows, HD), 1)
    table = jnp.zeros((rows, HD), F32)
    for i, column in enumerate(columns):
        table = jnp.where(lane == i, column, table)
    return table


def attend_own_kernel(held, k_low, v_low, own, own_log):
    _, low, causal = masks(own.shape[0])
    mask = jnp.logical_or(causal, low)
    heads = range(own.shape[1] // HD)
    own_log[...] = by_lane([attend_block(held, held, k_low, v_low, h, mask, own) for h in heads])


def attend_up_kernel(held, q_up, k_low, v_low, up):
    rows, width = q_up.shape
    here, low, _ = masks(rows)
    mask = jnp.logical_or(here, low)
    rest = [attend_block(q_up, held, k_low, v_low, h, mask, up) for h in range(width // HD)]
    terms = []
    for _ in range(3):
        high = [r.astype(BF16).astype(F32) for r in rest]
        rest = [r - t for r, t in zip(rest, high)]
        terms += high
    up[pl.ds(rows, 16), :] = jnp.zeros((16, width), BF16)
    up[pl.ds(rows, 16), pl.ds(0, HD)] = by_lane(terms).T[:16, :rows].astype(BF16)


def attend_own(held, k_low, v_low):
    rows, width = k_low.shape
    return pl.pallas_call(
        attend_own_kernel,
        out_shape=(
            jax.ShapeDtypeStruct((rows, width), F32),
            jax.ShapeDtypeStruct((rows, HD), F32),
        ),
        in_specs=[VMEM] * 3,
        out_specs=(VMEM,) * 2,
        compiler_params=pltpu.CompilerParams(vmem_limit_bytes=6 * 2**20),
    )(held, k_low, v_low)


def attend_up(held, q_up, k_low, v_low):
    rows, width = q_up.shape
    return pl.pallas_call(
        attend_up_kernel,
        out_shape=jax.ShapeDtypeStruct((rows + 16, width), BF16),
        in_specs=[VMEM] * 4,
        out_specs=VMEM,
        compiler_params=pltpu.CompilerParams(vmem_limit_bytes=6 * 2**20),
    )(held, q_up, k_low, v_low)


def copy_all(pairs, sems):
    copies = [pltpu.make_async_copy(a, b, sems.at[i]) for i, (a, b) in enumerate(pairs)]
    for copy in copies:
        copy.start()
    for copy in copies:
        copy.wait()


def hold_kernel(q, k, v, held):
    width = q.shape[1]
    for i, source in enumerate((q, k, v)):
        held[:, pl.ds(i * width, width)] = source[...]


def hold(q, k, v):
    return pl.pallas_call(
        hold_kernel,
        out_shape=jax.ShapeDtypeStruct((q.shape[0], 3 * q.shape[1]), q.dtype),
        in_specs=[VMEM] * 3,
        out_specs=VMEM,
        compiler_params=pltpu.CompilerParams(vmem_limit_bytes=2 * 2**20),
    )(q, k, v)


def bring_kernel(source, target, sems):
    rows = source.shape[0] // sems.shape[0]
    cuts = [pl.ds(i * rows, rows) for i in range(sems.shape[0])]
    copy_all([(source.at[c, :], target.at[c, :]) for c in cuts], sems)


def bring(x, parts):
    return pl.pallas_call(
        bring_kernel,
        out_shape=jax.ShapeDtypeStruct(x.shape, x.dtype),
        in_specs=[HBM],
        out_specs=VMEM,
        scratch_shapes=[pltpu.SemaphoreType.DMA((parts,))],
        compiler_params=pltpu.CompilerParams(vmem_limit_bytes=2 * 2**20),
    )(x)


def project_kernel(own, own_log, low, x, w, away, kept, attn, xs):
    ctx, dp, sub = lax.axis_index("ctx"), lax.axis_index("dp"), lax.axis_index("sub")
    rows, width = own.shape
    heads = width // HD
    quarter = rows // 4
    table = low[pl.ds(rows, 16), pl.ds(0, HD)].astype(F32)
    table = jnp.concatenate([table, jnp.zeros((HD - 16, HD), F32)], axis=0).T
    for h in range(heads):
        cols = pl.ds(h * HD, HD)
        log = own_log[:, h : h + 1]
        log_low = (
            table[:, h : h + 1]
            + table[:, heads + h : heads + h + 1]
            + table[:, 2 * heads + h : 2 * heads + h + 1]
        )
        log_low = jnp.where(ctx >= 2, log_low, -jnp.inf)
        top = jnp.maximum(log, log_low)
        share, share_low = jnp.exp(log - top), jnp.exp(log_low - top)
        mixed = share * own[:, cols] + share_low * low[pl.ds(0, rows), cols].astype(F32)
        attn[:, cols] = (mixed / (share + share_low)).astype(BF16)
    order = []
    for core in (1 - sub, sub):
        for chip in (1 - dp, dp):
            order.append(pl.ds(pl.multiple_of((chip * 2 + core) * quarter, quarter), quarter))
    a = jnp.concatenate([attn[o, :] for o in order], axis=0)
    for i, o in enumerate(order):
        xs[pl.ds(i * quarter, quarter), :] = x[o, :]
    block = x.shape[1]
    mine = dp * 2 + sub
    for b in range(w.shape[1] // block):
        cols = pl.ds(b * block, block)
        terms = dot(a, w[:, cols])
        terms += jnp.where(mine == b, xs[...].astype(F32), 0.0)
        away[:, cols] = terms[: 2 * quarter].astype(BF16)
        kept[:, cols] = terms[2 * quarter :]


def project(own, own_log, low, x, w):
    rows, width = own.shape
    half = rows // 2
    return pl.pallas_call(
        project_kernel,
        out_shape=(
            jax.ShapeDtypeStruct((half, w.shape[1]), BF16),
            jax.ShapeDtypeStruct((half, w.shape[1]), F32),
        ),
        in_specs=[VMEM] * 5,
        out_specs=(VMEM, VMEM),
        scratch_shapes=[pltpu.VMEM((rows, width), BF16), pltpu.VMEM(x.shape, BF16)],
        compiler_params=pltpu.CompilerParams(vmem_limit_bytes=12 * 2**20),
        cost_estimate=pl.CostEstimate(
            flops=2 * rows * width * w.shape[1],
            bytes_accessed=2 * w.size + 6 * half * w.shape[1],
            transcendentals=3 * rows * width // HD,
        ),
    )(own, own_log, low, x, w)


def sum_kernel(kept, away, send, stay):
    rows = send.shape[0]
    summed = kept[...] + away[...].astype(F32)
    send[...] = summed[:rows].astype(BF16)
    stay[...] = summed[rows:]


def sum_cores(kept, away):
    rows, width = kept.shape[0] // 2, kept.shape[1]
    return pl.pallas_call(
        sum_kernel,
        out_shape=(
            jax.ShapeDtypeStruct((rows, width), BF16),
            jax.ShapeDtypeStruct((rows, width), F32),
        ),
        in_specs=[VMEM] * 2,
        out_specs=(VMEM,) * 2,
        compiler_params=pltpu.CompilerParams(vmem_limit_bytes=2 * 2**20),
    )(kept, away)


def bytes_kernel(g0, g1, embed, gain, *refs):
    bridge, halves = refs[:2], refs[2:6]
    hid, turned, bw = refs[6:]
    dp, sub, grp = lax.axis_index("dp"), lax.axis_index("sub"), lax.axis_index("groups")
    patches = g0.shape[0]
    bytes_ = g0.shape[1] // DSLICE
    rows = patches * bytes_
    depth = bridge[0].shape[0]
    order = block_order(dp, sub)
    cut = halves[0].shape[0]
    for b, ref in zip(order[:2], bridge):
        bw[pl.ds(pl.multiple_of(b * depth, depth), depth), :] = ref[...]
    for i, ref in enumerate(halves):
        row = order[2 + i // 2] * depth + i % 2 * cut
        bw[pl.ds(pl.multiple_of(row, 32), ref.shape[0]), :] = ref[...]
    glob = (g0[...] + g1[...].astype(F32)).astype(BF16)
    stacked = jnp.concatenate(
        [glob[:, p * DSLICE : (p + 1) * DSLICE] for p in range(bytes_)], axis=0
    )
    to = lax.broadcasted_iota(jnp.int32, (rows, rows), 0)
    source = lax.broadcasted_iota(jnp.int32, (rows, rows), 1)
    pick = ((to % bytes_) * patches + to // bytes_ == source).astype(BF16)
    by_patch = dot(pick, stacked).astype(BF16)
    byte_in = embed[...].astype(F32) + dot(by_patch, bw[...])
    mean_square = jnp.mean(byte_in * byte_in, axis=1, keepdims=True)
    normalized = (byte_in * lax.rsqrt(mean_square + 1e-05) * gain[...]).astype(BF16)
    hid[...] = normalized
    half = normalized.shape[1] // 2
    turned[:, pl.ds(pl.multiple_of(grp * half, half), half)] = normalized[:, :half]
    turned[:, pl.ds(pl.multiple_of((1 - grp) * half, half), half)] = normalized[:, half:]


def block_order(dp, sub):
    return [dp * 2 + sub, dp * 2 + 1 - sub, (1 - dp) * 2 + sub, (1 - dp) * 2 + 1 - sub]


def bytes_in(g0, g1, embed, gain, bridge):
    rows = embed.shape[0]
    return pl.pallas_call(
        bytes_kernel,
        out_shape=(jax.ShapeDtypeStruct((rows, DL), BF16),) * 2,
        in_specs=[VMEM] * 10,
        out_specs=(VMEM,) * 2,
        scratch_shapes=[pltpu.VMEM((DSLICE, DL), BF16)],
        compiler_params=pltpu.CompilerParams(vmem_limit_bytes=10 * 2**20),
        cost_estimate=pl.CostEstimate(
            flops=2 * rows * DL * DSLICE, bytes_accessed=6 * rows * DL, transcendentals=rows
        ),
    )(g0, g1, embed, gain, *bridge)


def project_pieces(source, refs):
    total, row = None, 0
    for ref in refs:
        term = dot(source[:, row : row + ref.shape[0]], ref[...])
        total = term if total is None else total + term
        row += ref.shape[0]
    return total.astype(BF16)


def first_blocks_kernel(hid, turned, *refs, counts):
    out, at = refs[-1], 0
    for i, count in enumerate(counts):
        out[i, :, :] = project_pieces(hid if count == 1 else turned, refs[at : at + count])
        at += count


def last_block_kernel(turned, first, *refs):
    pieces, (out, held, sems) = refs[:-3], refs[-3:]
    width = held.shape[1]
    order = block_order(lax.axis_index("dp"), lax.axis_index("sub"))
    copies = []
    for i, b in enumerate(order):
        if i == len(order) - 1:
            held[...] = project_pieces(turned, pieces)
        copy = pltpu.make_async_copy(
            first.at[i] if i < len(order) - 1 else held,
            out.at[:, pl.ds(pl.multiple_of(b * width, 128), width)],
            sems.at[i],
        )
        copy.start()
        copies.append(copy)
    for copy in copies:
        copy.wait()


def local(hid, turned, *blocks):
    rows = hid.shape[0]
    weights = [piece for block in blocks[:-1] for piece in block]
    width = weights[0].shape[1]
    first = pl.pallas_call(
        functools.partial(
            first_blocks_kernel, counts=tuple(len(block) for block in blocks[:-1])
        ),
        out_shape=jax.ShapeDtypeStruct((len(blocks) - 1, rows, width), BF16),
        in_specs=[VMEM] * (2 + len(weights)),
        out_specs=VMEM,
        compiler_params=pltpu.CompilerParams(vmem_limit_bytes=12 * 2**20),
    )(hid, turned, *weights)
    return pl.pallas_call(
        last_block_kernel,
        out_shape=jax.ShapeDtypeStruct((rows, len(blocks) * width), BF16),
        in_specs=[VMEM] * (2 + len(blocks[-1])),
        out_specs=pl.BlockSpec(memory_space=pl.ANY),
        scratch_shapes=[
            pltpu.VMEM((rows, width), BF16),
            pltpu.SemaphoreType.DMA((len(blocks),)),
        ],
        compiler_params=pltpu.CompilerParams(vmem_limit_bytes=12 * 2**20),
    )(turned, first, *blocks[-1])


def swap(x, axis):
    return lax.ppermute(x, axis, [(0, 1), (1, 0)])


def after(x, *events):
    return lax.optimization_barrier((x, *events))[0]


def small_mesh(
    q_glob, k_glob, v_glob, x_glob, out_weight, bridge_weight, byte_embed, norm_gain, qkv_weight
):
    grp = lax.axis_index("groups")

    quarter = qkv_weight.shape[0] // 4
    held = hold(q_glob, k_glob, v_glob)
    w0 = lax.dynamic_slice_in_dim(qkv_weight, grp * 2 * quarter, quarter, 0)
    w1 = lax.dynamic_slice_in_dim(after(qkv_weight, held), (grp * 2 + 1) * quarter, quarter, 0)

    x0 = swap(w0, "dp")
    bridge_rows = bridge_weight.shape[0] // 4 * 3
    bridge_a = swap(bridge_weight[:bridge_rows], "dp")
    q_up = lax.ppermute(q_glob, "ctx", [(2, 0), (3, 1)])
    k_low = lax.ppermute(k_glob, "ctx", [(0, 1), (1, 2), (2, 3)])
    v_low = lax.ppermute(v_glob, "ctx", [(0, 1), (1, 2), (2, 3)])
    q_up, k_low, v_low, x0, bridge_a, held, w1, bridge_weight, qkv_weight = (
        lax.optimization_barrier(
            (q_up, k_low, v_low, x0, bridge_a, held, w1, bridge_weight, qkv_weight)
        )
    )

    up = attend_up(held, q_up, k_low, v_low)
    own, own_log = attend_own(held, k_low, v_low)
    low = lax.ppermute(up, "ctx", [(0, 2), (1, 3)])
    x1 = swap(w1, "dp")
    y0 = swap(x0, "groups")
    other_core = swap(qkv_weight, "sub")
    out_weight = bring(after(out_weight, up), 4)
    bridge_b = swap(bridge_weight[bridge_rows:], "dp")
    low, x0, x1, other_core, out_weight, bridge_a, bridge_b = lax.optimization_barrier(
        (low, x0, x1, other_core, out_weight, bridge_a, bridge_b)
    )

    away, kept = project(own, own_log, low, x_glob, out_weight)
    away = swap(away, "sub")
    y1 = swap(x1, "groups")
    core_bridge_a = swap(bridge_a, "sub")
    core_bridge_b = swap(bridge_b, "sub")
    core_y0 = swap(y0, "sub")
    away, core_y0, core_bridge_a, core_bridge_b, x0, x1, bridge_weight = lax.optimization_barrier(
        (away, core_y0, core_bridge_a, core_bridge_b, x0, x1, bridge_weight)
    )

    send, stay = sum_cores(kept, away)
    across = swap(send, "dp")
    core_x1 = swap(x1, "sub")
    bridge_core = swap(bridge_weight, "sub")
    core_x0 = swap(x0, "sub")
    across, y1, core_x0, core_x1, bridge_core = lax.optimization_barrier(
        (across, y1, core_x0, core_x1, bridge_core)
    )

    core_y1 = swap(y1, "sub")
    rows = byte_embed.shape[0] * byte_embed.shape[1]
    hidden, turned = bytes_in(
        stay,
        across,
        byte_embed.reshape(rows, DL),
        norm_gain.reshape(1, DL),
        [bridge_weight, bridge_core, bridge_a, bridge_b, core_bridge_a, core_bridge_b],
    )
    result = local(
        hidden,
        turned,
        [qkv_weight],
        [other_core],
        [x0, x1, y0, y1],
        [core_x0, core_x1, core_y0, core_y1],
    )
    return result.reshape(byte_embed.shape[0], P_SIZE, result.shape[1])


def solution(mesh):
    rows = P(("groups", "ctx"), GROUP)
    in_specs = (
        rows,
        rows,
        rows,
        rows,
        P(GROUP, None),
        P(GROUP, None),
        P(("groups", "ctx", "dp", "sub"), None, None),
        P(),
        P(None, GROUP),
    )
    out_specs = P(("groups", "ctx", "dp", "sub"), None, None)
    pairs = all(mesh.shape[a] == 2 for a in ("groups", "dp", "sub"))
    per_device = small_mesh if pairs and mesh.shape["ctx"] == 4 else any_mesh
    return jax.shard_map(
        per_device, mesh=mesh, in_specs=in_specs, out_specs=out_specs, check_vma=False
    )
```

```python
import functools
import math

import jax
import jax.numpy as jnp
from jax import lax
from jax.experimental import pallas as pl
from jax.experimental.pallas import tpu as pltpu
from jax.sharding import PartitionSpec as P

HD = 128
DL = 1024
P_SIZE = 8
DSLICE = 512
GROUP = ("dp", "sub")
SCALE = 1.0 / math.sqrt(HD)
VMEM = pl.BlockSpec(memory_space=pltpu.VMEM)
HBM = pl.BlockSpec(memory_space=pltpu.HBM)
F32 = jnp.float32
BF16 = jnp.bfloat16


def dot(a, b):
    return jnp.dot(a, b, preferred_element_type=F32)


def any_mesh(
    q_glob, k_glob, v_glob, x_glob, out_weight, bridge_weight, byte_embed, norm_gain, qkv_weight
):
    query_rows, query_width = q_glob.shape
    head_count = query_width // HD
    first_row = lax.axis_index("ctx") * query_rows
    queries = q_glob.reshape(query_rows, head_count, HD)
    query_pos = first_row + lax.iota(jnp.int32, query_rows)
    keys = lax.all_gather(k_glob, "ctx", axis=0, tiled=True)
    values = lax.all_gather(v_glob, "ctx", axis=0, tiled=True)
    count = keys.shape[0]
    keys = keys.reshape(count, head_count, HD)
    values = values.reshape(count, head_count, HD)
    scores = jnp.einsum("qhd,khd->hqk", queries, keys, preferred_element_type=F32) * SCALE
    allowed = query_pos[:, None] >= lax.iota(jnp.int32, count)[None, :]
    scores = jnp.where(allowed[None], scores, -jnp.inf)
    weights = jnp.exp(scores - jnp.max(scores, axis=2)[:, :, None])
    row_sum = jnp.sum(weights, axis=2)
    weighted = jnp.einsum("hqk,khd->hqd", weights.astype(BF16), values, preferred_element_type=F32)
    attn = (weighted / row_sum[:, :, None]).astype(BF16)
    attn = attn.transpose(1, 0, 2).reshape(query_rows, query_width)
    head_terms = dot(attn, out_weight)
    own_bytes = P_SIZE // lax.axis_size(GROUP)
    feature_sum = lax.psum_scatter(
        head_terms.astype(BF16), GROUP, scatter_dimension=1, tiled=True
    ).astype(F32)
    patch_out = (feature_sum + x_glob.astype(F32)).astype(BF16)
    patch_out = patch_out.reshape(query_rows, own_bytes, DSLICE)
    patch_out = lax.all_to_all(patch_out, GROUP, split_axis=0, concat_axis=1, tiled=True)
    glob_bytes = patch_out.reshape(-1, DSLICE)
    byte_rows = glob_bytes.shape[0]
    bridged = dot(glob_bytes, lax.all_gather(bridge_weight, GROUP, axis=0, tiled=True))
    byte_in = byte_embed.reshape(byte_rows, DL).astype(F32) + bridged
    mean_square = jnp.mean(byte_in * byte_in, axis=1, keepdims=True)
    normalized = (byte_in * lax.rsqrt(mean_square + 1e-05) * norm_gain).astype(BF16)
    result = dot(normalized, lax.all_gather(qkv_weight, GROUP, axis=1, tiled=True)).astype(BF16)
    return result.reshape(byte_embed.shape[0], P_SIZE, 3 * DL)


def attend_block(queries, held, k_low, v_low, h, mask, target):
    rows = queries.shape[0]
    width = k_low.shape[1]
    cols = pl.ds(h * HD, HD)
    k, v = (held[:, pl.ds(i * width + h * HD, HD)] for i in (1, 2))
    kh = jnp.concatenate([k, k_low[:, cols]], axis=0)
    vh = jnp.concatenate([v, v_low[:, cols]], axis=0)
    scores = lax.dot_general(
        queries[:, cols], kh, (((1,), (1,)), ((), ())), preferred_element_type=F32
    ) * SCALE
    scores = jnp.where(mask, scores, -jnp.inf)
    top = jnp.max(scores, axis=1, keepdims=True)
    probs = jnp.exp(scores - top)
    total = jnp.sum(probs, axis=1, keepdims=True)
    mixed = dot(probs.astype(BF16), vh) / total
    target[pl.ds(0, rows), cols] = mixed.astype(target.dtype)
    return top + jnp.log(total)


def masks(rows):
    row = lax.broadcasted_iota(jnp.int32, (rows, 2 * rows), 0)
    col = lax.broadcasted_iota(jnp.int32, (rows, 2 * rows), 1)
    low = jnp.logical_and(col >= rows, lax.axis_index("ctx") >= 1)
    return col < rows, low, row >= col


def by_lane(columns):
    rows = columns[0].shape[0]
    lane = lax.broadcasted_iota(jnp.int32, (rows, HD), 1)
    table = jnp.zeros((rows, HD), F32)
    for i, column in enumerate(columns):
        table = jnp.where(lane == i, column, table)
    return table


def attend_own_kernel(held, k_low, v_low, own, own_log):
    _, low, causal = masks(own.shape[0])
    mask = jnp.logical_or(causal, low)
    heads = range(own.shape[1] // HD)
    own_log[...] = by_lane([attend_block(held, held, k_low, v_low, h, mask, own) for h in heads])


def attend_up_kernel(held, q_up, k_low, v_low, up):
    rows, width = q_up.shape
    here, low, _ = masks(rows)
    mask = jnp.logical_or(here, low)
    rest = [attend_block(q_up, held, k_low, v_low, h, mask, up) for h in range(width // HD)]
    terms = []
    for _ in range(3):
        high = [r.astype(BF16).astype(F32) for r in rest]
        rest = [r - t for r, t in zip(rest, high)]
        terms += high
    up[pl.ds(rows, 16), :] = jnp.zeros((16, width), BF16)
    up[pl.ds(rows, 16), pl.ds(0, HD)] = by_lane(terms).T[:16, :rows].astype(BF16)


def attend_own(held, k_low, v_low):
    rows, width = k_low.shape
    return pl.pallas_call(
        attend_own_kernel,
        out_shape=(
            jax.ShapeDtypeStruct((rows, width), F32),
            jax.ShapeDtypeStruct((rows, HD), F32),
        ),
        in_specs=[VMEM] * 3,
        out_specs=(VMEM,) * 2,
        compiler_params=pltpu.CompilerParams(vmem_limit_bytes=6 * 2**20),
    )(held, k_low, v_low)


def attend_up(held, q_up, k_low, v_low):
    rows, width = q_up.shape
    return pl.pallas_call(
        attend_up_kernel,
        out_shape=jax.ShapeDtypeStruct((rows + 16, width), BF16),
        in_specs=[VMEM] * 4,
        out_specs=VMEM,
        compiler_params=pltpu.CompilerParams(vmem_limit_bytes=6 * 2**20),
    )(held, q_up, k_low, v_low)


def copy_all(pairs, sems):
    copies = [pltpu.make_async_copy(a, b, sems.at[i]) for i, (a, b) in enumerate(pairs)]
    for copy in copies:
        copy.start()
    for copy in copies:
        copy.wait()


def hold_kernel(q, k, v, held):
    width = q.shape[1]
    for i, source in enumerate((q, k, v)):
        held[:, pl.ds(i * width, width)] = source[...]


def hold(q, k, v):
    return pl.pallas_call(
        hold_kernel,
        out_shape=jax.ShapeDtypeStruct((q.shape[0], 3 * q.shape[1]), q.dtype),
        in_specs=[VMEM] * 3,
        out_specs=VMEM,
        compiler_params=pltpu.CompilerParams(vmem_limit_bytes=2 * 2**20),
    )(q, k, v)


def bring_kernel(source, target, sems):
    rows = source.shape[0] // sems.shape[0]
    cuts = [pl.ds(i * rows, rows) for i in range(sems.shape[0])]
    copy_all([(source.at[c, :], target.at[c, :]) for c in cuts], sems)


def bring(x, parts):
    return pl.pallas_call(
        bring_kernel,
        out_shape=jax.ShapeDtypeStruct(x.shape, x.dtype),
        in_specs=[HBM],
        out_specs=VMEM,
        scratch_shapes=[pltpu.SemaphoreType.DMA((parts,))],
        compiler_params=pltpu.CompilerParams(vmem_limit_bytes=2 * 2**20),
    )(x)


def project_kernel(own, own_log, low, x, w, away, kept, attn, xs):
    ctx, dp, sub = lax.axis_index("ctx"), lax.axis_index("dp"), lax.axis_index("sub")
    rows, width = own.shape
    heads = width // HD
    quarter = rows // 4
    table = low[pl.ds(rows, 16), pl.ds(0, HD)].astype(F32)
    table = jnp.concatenate([table, jnp.zeros((HD - 16, HD), F32)], axis=0).T
    for h in range(heads):
        cols = pl.ds(h * HD, HD)
        log = own_log[:, h : h + 1]
        log_low = (
            table[:, h : h + 1]
            + table[:, heads + h : heads + h + 1]
            + table[:, 2 * heads + h : 2 * heads + h + 1]
        )
        log_low = jnp.where(ctx >= 2, log_low, -jnp.inf)
        top = jnp.maximum(log, log_low)
        share, share_low = jnp.exp(log - top), jnp.exp(log_low - top)
        mixed = share * own[:, cols] + share_low * low[pl.ds(0, rows), cols].astype(F32)
        attn[:, cols] = (mixed / (share + share_low)).astype(BF16)
    order = []
    for core in (1 - sub, sub):
        for chip in (1 - dp, dp):
            order.append(pl.ds(pl.multiple_of((chip * 2 + core) * quarter, quarter), quarter))
    a = jnp.concatenate([attn[o, :] for o in order], axis=0)
    for i, o in enumerate(order):
        xs[pl.ds(i * quarter, quarter), :] = x[o, :]
    block = x.shape[1]
    mine = dp * 2 + sub
    for b in range(w.shape[1] // block):
        cols = pl.ds(b * block, block)
        terms = dot(a, w[:, cols])
        terms += jnp.where(mine == b, xs[...].astype(F32), 0.0)
        away[:, cols] = terms[: 2 * quarter].astype(BF16)
        kept[:, cols] = terms[2 * quarter :]


def project(own, own_log, low, x, w):
    rows, width = own.shape
    half = rows // 2
    return pl.pallas_call(
        project_kernel,
        out_shape=(
            jax.ShapeDtypeStruct((half, w.shape[1]), BF16),
            jax.ShapeDtypeStruct((half, w.shape[1]), F32),
        ),
        in_specs=[VMEM] * 5,
        out_specs=(VMEM, VMEM),
        scratch_shapes=[pltpu.VMEM((rows, width), BF16), pltpu.VMEM(x.shape, BF16)],
        compiler_params=pltpu.CompilerParams(vmem_limit_bytes=12 * 2**20),
        cost_estimate=pl.CostEstimate(
            flops=2 * rows * width * w.shape[1],
            bytes_accessed=2 * w.size + 6 * half * w.shape[1],
            transcendentals=3 * rows * width // HD,
        ),
    )(own, own_log, low, x, w)


def sum_kernel(kept, away, send, stay):
    rows = send.shape[0]
    summed = kept[...] + away[...].astype(F32)
    send[...] = summed[:rows].astype(BF16)
    stay[...] = summed[rows:]


def sum_cores(kept, away):
    rows, width = kept.shape[0] // 2, kept.shape[1]
    return pl.pallas_call(
        sum_kernel,
        out_shape=(
            jax.ShapeDtypeStruct((rows, width), BF16),
            jax.ShapeDtypeStruct((rows, width), F32),
        ),
        in_specs=[VMEM] * 2,
        out_specs=(VMEM,) * 2,
        compiler_params=pltpu.CompilerParams(vmem_limit_bytes=2 * 2**20),
    )(kept, away)


def bytes_kernel(g0, g1, embed, gain, *refs):
    bridge, halves = refs[:2], refs[2:6]
    hid, turned, bw = refs[6:]
    dp, sub, grp = lax.axis_index("dp"), lax.axis_index("sub"), lax.axis_index("groups")
    patches = g0.shape[0]
    bytes_ = g0.shape[1] // DSLICE
    rows = patches * bytes_
    depth = bridge[0].shape[0]
    order = block_order(dp, sub)
    cut = halves[0].shape[0]
    for b, ref in zip(order[:2], bridge):
        bw[pl.ds(pl.multiple_of(b * depth, depth), depth), :] = ref[...]
    for i, ref in enumerate(halves):
        row = order[2 + i // 2] * depth + i % 2 * cut
        bw[pl.ds(pl.multiple_of(row, 16), ref.shape[0]), :] = ref[...]
    glob = (g0[...] + g1[...].astype(F32)).astype(BF16)
    stacked = jnp.concatenate(
        [glob[:, p * DSLICE : (p + 1) * DSLICE] for p in range(bytes_)], axis=0
    )
    to = lax.broadcasted_iota(jnp.int32, (rows, rows), 0)
    source = lax.broadcasted_iota(jnp.int32, (rows, rows), 1)
    pick = ((to % bytes_) * patches + to // bytes_ == source).astype(BF16)
    by_patch = dot(pick, stacked).astype(BF16)
    byte_in = embed[...].astype(F32) + dot(by_patch, bw[...])
    mean_square = jnp.mean(byte_in * byte_in, axis=1, keepdims=True)
    normalized = (byte_in * lax.rsqrt(mean_square + 1e-05) * gain[...]).astype(BF16)
    hid[...] = normalized
    half = normalized.shape[1] // 2
    turned[:, pl.ds(pl.multiple_of(grp * half, half), half)] = normalized[:, :half]
    turned[:, pl.ds(pl.multiple_of((1 - grp) * half, half), half)] = normalized[:, half:]


def block_order(dp, sub):
    return [dp * 2 + sub, dp * 2 + 1 - sub, (1 - dp) * 2 + sub, (1 - dp) * 2 + 1 - sub]


def bytes_in(g0, g1, embed, gain, bridge):
    rows = embed.shape[0]
    return pl.pallas_call(
        bytes_kernel,
        out_shape=(jax.ShapeDtypeStruct((rows, DL), BF16),) * 2,
        in_specs=[VMEM] * 10,
        out_specs=(VMEM,) * 2,
        scratch_shapes=[pltpu.VMEM((DSLICE, DL), BF16)],
        compiler_params=pltpu.CompilerParams(vmem_limit_bytes=10 * 2**20),
        cost_estimate=pl.CostEstimate(
            flops=2 * rows * DL * DSLICE, bytes_accessed=6 * rows * DL, transcendentals=rows
        ),
    )(g0, g1, embed, gain, *bridge)


def project_pieces(source, refs):
    total, row = None, 0
    for ref in refs:
        term = dot(source[:, row : row + ref.shape[0]], ref[...])
        total = term if total is None else total + term
        row += ref.shape[0]
    return total.astype(BF16)


def first_blocks_kernel(hid, turned, *refs, counts):
    out, at = refs[-1], 0
    for i, count in enumerate(counts):
        out[i, :, :] = project_pieces(hid if count == 1 else turned, refs[at : at + count])
        at += count


def last_block_kernel(turned, first, *refs):
    pieces, (out, held, sems) = refs[:-3], refs[-3:]
    width = first.shape[2]
    order = block_order(lax.axis_index("dp"), lax.axis_index("sub"))
    copies = []
    last = len(order) - 1
    for i, b in enumerate(order[:last]):
        columns = pl.ds(pl.multiple_of(b * width, 128), width)
        copies.append(pltpu.make_async_copy(first.at[i], out.at[:, columns], sems.at[i]))
        copies[-1].start()
    half = width // 2
    for i in range(2):
        cut = pl.ds(i * half, half)
        held[i, :, :] = project_pieces(turned, [piece.at[:, cut] for piece in pieces])
        columns = pl.ds(pl.multiple_of(order[last] * width + i * half, 128), half)
        copies.append(pltpu.make_async_copy(held.at[i], out.at[:, columns], sems.at[last + i]))
        copies[-1].start()
    for copy in copies:
        copy.wait()


def local(hid, turned, *blocks):
    rows = hid.shape[0]
    weights = [piece for block in blocks[:-1] for piece in block]
    width = weights[0].shape[1]
    first = pl.pallas_call(
        functools.partial(
            first_blocks_kernel, counts=tuple(len(block) for block in blocks[:-1])
        ),
        out_shape=jax.ShapeDtypeStruct((len(blocks) - 1, rows, width), BF16),
        in_specs=[VMEM] * (2 + len(weights)),
        out_specs=VMEM,
        compiler_params=pltpu.CompilerParams(vmem_limit_bytes=12 * 2**20),
    )(hid, turned, *weights)
    return pl.pallas_call(
        last_block_kernel,
        out_shape=jax.ShapeDtypeStruct((rows, len(blocks) * width), BF16),
        in_specs=[VMEM] * (2 + len(blocks[-1])),
        out_specs=pl.BlockSpec(memory_space=pl.ANY),
        scratch_shapes=[
            pltpu.VMEM((2, rows, width // 2), BF16),
            pltpu.SemaphoreType.DMA((len(blocks) + 1,)),
        ],
        compiler_params=pltpu.CompilerParams(vmem_limit_bytes=12 * 2**20),
    )(turned, first, *blocks[-1])


def swap(x, axis):
    return lax.ppermute(x, axis, [(0, 1), (1, 0)])


def after(x, *events):
    return lax.optimization_barrier((x, *events))[0]


def small_mesh(
    q_glob, k_glob, v_glob, x_glob, out_weight, bridge_weight, byte_embed, norm_gain, qkv_weight
):
    grp = lax.axis_index("groups")

    quarter = qkv_weight.shape[0] // 4
    held = hold(q_glob, k_glob, v_glob)
    w0 = lax.dynamic_slice_in_dim(qkv_weight, grp * 2 * quarter, quarter, 0)
    w1 = lax.dynamic_slice_in_dim(after(qkv_weight, held), (grp * 2 + 1) * quarter, quarter, 0)

    x0 = swap(w0, "dp")
    bridge_rows = bridge_weight.shape[0] // 8 * 5
    bridge_a = swap(bridge_weight[:bridge_rows], "dp")
    q_up = lax.ppermute(q_glob, "ctx", [(2, 0), (3, 1)])
    k_low = lax.ppermute(k_glob, "ctx", [(0, 1), (1, 2), (2, 3)])
    v_low = lax.ppermute(v_glob, "ctx", [(0, 1), (1, 2), (2, 3)])
    q_up, k_low, v_low, x0, bridge_a, held, w1, bridge_weight, qkv_weight = (
        lax.optimization_barrier(
            (q_up, k_low, v_low, x0, bridge_a, held, w1, bridge_weight, qkv_weight)
        )
    )

    up = attend_up(held, q_up, k_low, v_low)
    own, own_log = attend_own(held, k_low, v_low)
    low = lax.ppermute(up, "ctx", [(0, 2), (1, 3)])
    x1 = swap(w1, "dp")
    y0 = swap(x0, "groups")
    other_core = swap(qkv_weight, "sub")
    out_weight = bring(after(out_weight, up), 4)
    bridge_b = swap(bridge_weight[bridge_rows:], "dp")
    low, x0, x1, other_core, out_weight, bridge_a, bridge_b = lax.optimization_barrier(
        (low, x0, x1, other_core, out_weight, bridge_a, bridge_b)
    )

    away, kept = project(own, own_log, low, x_glob, out_weight)
    away = swap(away, "sub")
    y1 = swap(x1, "groups")
    core_bridge_a = swap(bridge_a, "sub")
    core_bridge_b = swap(bridge_b, "sub")
    core_y0 = swap(y0, "sub")
    away, core_y0, core_bridge_a, core_bridge_b, x0, x1, bridge_weight = lax.optimization_barrier(
        (away, core_y0, core_bridge_a, core_bridge_b, x0, x1, bridge_weight)
    )

    send, stay = sum_cores(kept, away)
    across = swap(send, "dp")
    core_x1 = swap(x1, "sub")
    bridge_core = swap(bridge_weight, "sub")
    core_x0 = swap(x0, "sub")
    across, y1, core_x0, core_x1, bridge_core = lax.optimization_barrier(
        (across, y1, core_x0, core_x1, bridge_core)
    )

    core_y1 = swap(y1, "sub")
    rows = byte_embed.shape[0] * byte_embed.shape[1]
    hidden, turned = bytes_in(
        stay,
        across,
        byte_embed.reshape(rows, DL),
        norm_gain.reshape(1, DL),
        [bridge_weight, bridge_core, bridge_a, bridge_b, core_bridge_a, core_bridge_b],
    )
    result = local(
        hidden,
        turned,
        [qkv_weight],
        [other_core],
        [x0, x1, y0, y1],
        [core_x0, core_x1, core_y0, core_y1],
    )
    return result.reshape(byte_embed.shape[0], P_SIZE, result.shape[1])


def solution(mesh):
    rows = P(("groups", "ctx"), GROUP)
    in_specs = (
        rows,
        rows,
        rows,
        rows,
        P(GROUP, None),
        P(GROUP, None),
        P(("groups", "ctx", "dp", "sub"), None, None),
        P(),
        P(None, GROUP),
    )
    out_specs = P(("groups", "ctx", "dp", "sub"), None, None)
    pairs = all(mesh.shape[a] == 2 for a in ("groups", "dp", "sub"))
    per_device = small_mesh if pairs and mesh.shape["ctx"] == 4 else any_mesh
    return jax.shard_map(
        per_device, mesh=mesh, in_specs=in_specs, out_specs=out_specs, check_vma=False
    )
```
